128 devices in a mesh: lon: 32 (over x, z, y_lo), lat: 4 (over y_hi, core).
Axes of the slice: x: 4, y: 4 (y_hi: 2, y_lo: 2; y = y_hi * 2 + y_lo), z: 4, core: 2. Of those that a mesh axis runs over, the one named last changes fastest.
Arguments:
- latent: bfloat16 [64, 1024, 640], P('lat', 'lon'), may hold values from -6 to 6
- stale: bfloat16 [64, 1024, 640], P('lat', 'lon'), may hold values from -6 to 6
- stale_kv: bfloat16 [2, 64, 1024, 640], P(None, 'lat', 'lon'), may hold values from -600 to 600
- neighbors: int32 [4, 32, 2], replicated, may hold values from -1 to 31, as said below
- readers: int32 [4, 32, 6], replicated, may hold values from -1 to 31, as said below
- timestep: int32 [1], replicated, may hold values from 0 to 999
- conv_weight: bfloat16 [3, 3, 640, 640], replicated, may hold values from -0.078125 to 0.078125
- time_weight: float32 [320, 640], replicated, may hold values from -0.3125 to 0.3125
- norm_gain: float32 [640], replicated, may hold values from 0.1 to 1.9
- qkv_weight: bfloat16 [640, 1920], replicated, may hold values from -0.25 to 0.25
- out_weight: bfloat16 [640, 640], replicated, may hold values from -0.25 to 0.25
Outputs:
- block_out: bfloat16 [64, 1024, 640], P('lat', 'lon')
- fresh_kv: bfloat16 [2, 64, 1024, 640], P(None, 'lat', 'lon')
The draws below stay inside these ranges and needn't reach their ends.
Inputs may be any that keep to these rules, and one draw needn't show every extreme that they name: `neighbors`: entry 0 names a patch of the band above, entry 1 of the band below; -1 exactly at the top band's entry 0 and the bottom band's entry 1. Within one band, every patch's entry equals its own longitude index plus one shift of that band, modulo the number of longitude patches. `readers`: readers belong to the tile's own band and lie within 3 longitude patches of the tile around the loop, never the tile's own patch; unused slots hold -1. Tiles of the two polar bands are read from distance 1 and 3; tiles of the two inner bands are read from distance 1 and never from distance 3.
All inputs are finite; a program needn't handle non-finite values.
Results may differ from the reference program's by a relative error of at most 0.0065.
Values may be sent and summed in bfloat16 or wider, within the bound.
No kernel may reach another device: no remote copies, remote signals or barrier semaphores. Data moves between devices by JAX's collectives and lax.ppermute only.
A program may use at most 256 MiB of HBM per device.

```python
import math
import jax
import jax.numpy as jnp
from jax import lax

LAT_CELLS = 16
LON_CELLS = 32
CHANNELS = 640
HEAD_COUNT = 10
HEAD_SIZE = 64
TIME_WIDTH = 320
REACH_TILES = 3
TOTAL_LAT = 64
TOTAL_LON = 1024
N_LON = 32
N_LAT = 4


def draw_stale_kv(key, part):
    key = jax.random.fold_in(key, 11)
    shape = (2, LAT_CELLS * N_LAT, LON_CELLS * N_LON, CHANNELS)
    base = jnp.clip(jax.random.normal(key, shape, jnp.float32), -6.0, 6.0)
    return base.astype(jnp.bfloat16)


def draw_neighbors(key, part):
    key = jax.random.fold_in(key, 5)
    shifts = jax.random.randint(key, (N_LAT,), 0, N_LON)
    shifts = shifts.at[1].set(jnp.mod(shifts[0] + N_LON // 2, N_LON))
    position = jnp.arange(N_LON)[None, :]
    north_link = jnp.mod(position + shifts[:, None] - jnp.roll(shifts, 1)[:, None], N_LON)
    south_link = jnp.mod(position + shifts[:, None] - jnp.roll(shifts, -1)[:, None], N_LON)
    band_rows = jnp.arange(N_LAT)[:, None]
    north_link = jnp.where(band_rows == 0, -1, north_link)
    south_link = jnp.where(band_rows == N_LAT - 1, -1, south_link)
    return jnp.stack([north_link, south_link], -1).astype(jnp.int32)


def draw_readers(key, part):
    key = jax.random.fold_in(key, 7)
    offsets = jnp.concatenate([jnp.arange(-REACH_TILES, 0), jnp.arange(1, REACH_TILES + 1)])
    coins = jax.random.randint(key, (N_LAT, N_LON, 2 * REACH_TILES), 0, 2)
    band_rows = jnp.arange(N_LAT)[:, None, None]
    polar = (band_rows == 0) | (band_rows == N_LAT - 1)
    distance = jnp.abs(offsets)[None, None, :]
    polar_keep = (distance == 1) | (distance == REACH_TILES) | (coins == 1)
    inner_keep = (distance == 1) | (distance == 2) & (coins == 1)
    keeping = jnp.where(polar, polar_keep, inner_keep)
    tile_pos = jnp.arange(N_LON)[None, :, None]
    reader_pos = jnp.mod(tile_pos - offsets[None, None, :], N_LON)
    return jnp.where(keeping, reader_pos, -1).astype(jnp.int32)


def block_levels(stream_key, dims, split, low, high):
    level = 1.0
    for axis_at, shards_of in split:
        draws = jax.random.uniform(jax.random.fold_in(jax.random.fold_in(stream_key, 6), axis_at), (shards_of,), jnp.float32, low / len(split), high / len(split))
        level = level * jnp.repeat(jnp.exp(draws), dims[axis_at] // shards_of).reshape((-1,) + (1,) * (len(dims) - 1 - axis_at))
    return level


def centred(key, dims, scale, limit, pieces=(), kind=jnp.bfloat16):
    values = scale * jax.random.normal(key, dims, jnp.float32)
    if pieces:
        values = values * block_levels(key, dims, pieces, -0.22, 0.18)
    return jnp.clip(values, -limit, limit).astype(kind)


def setup_inputs(seed: int = 0) -> dict:
    splits = jax.random.split(jax.random.key(seed), 12)
    latent = centred(splits[0], (TOTAL_LAT, TOTAL_LON, CHANNELS), 1.0, 6.0, ((0, 4), (1, 32)))
    stale = centred(splits[1], (TOTAL_LAT, TOTAL_LON, CHANNELS), 1.0, 6.0, ((0, 4), (1, 32)))
    stale_kv = draw_stale_kv(jax.random.fold_in(splits[11], 71), 0)
    neighbors = draw_neighbors(jax.random.fold_in(splits[11], 71), 0)
    readers = draw_readers(jax.random.fold_in(splits[11], 71), 0)
    timestep = jax.random.randint(splits[5], (1,), 0, 1000).astype(jnp.int32)
    conv_weight = centred(splits[6], (3, 3, CHANNELS, CHANNELS), (9 * CHANNELS) ** -0.5, 0.078125)
    time_weight = centred(splits[7], (TIME_WIDTH, CHANNELS), TIME_WIDTH ** -0.5, 0.3125, (), jnp.float32)
    norm_gain = jnp.clip(1.0 + 0.18 * jax.random.normal(splits[8], (CHANNELS,), jnp.float32), 0.1, 1.9)
    qkv_weight = centred(splits[9], (CHANNELS, 3 * CHANNELS), CHANNELS ** -0.5, 0.25)
    out_weight = centred(splits[10], (CHANNELS, CHANNELS), CHANNELS ** -0.5, 0.25)
    return dict(latent=latent, stale=stale, stale_kv=stale_kv, neighbors=neighbors, readers=readers, timestep=timestep, conv_weight=conv_weight, time_weight=time_weight, norm_gain=norm_gain, qkv_weight=qkv_weight, out_weight=out_weight)


norm_epsilon = 1e-05
attention_scale = 0.125

def to_patches(whole):
    width = whole.shape[-1]
    return whole.reshape(N_LAT, LAT_CELLS, N_LON, LON_CELLS, width).transpose(0, 2, 1, 3, 4)

def from_patches(blocks):
    width = blocks.shape[-1]
    return blocks.transpose(0, 2, 1, 3, 4).reshape(N_LAT * LAT_CELLS, N_LON * LON_CELLS, width)

def time_vector(timestep, time_weight):
    half_width = TIME_WIDTH // 2
    frequency = jnp.exp(-math.log(10000.0) * jnp.arange(half_width, dtype=jnp.float32) / half_width)
    angles = timestep.astype(jnp.float32)[0] * frequency
    embedding = jnp.concatenate([jnp.cos(angles), jnp.sin(angles)])
    return jnp.dot(embedding[None, :], time_weight, precision=lax.Precision.HIGHEST, preferred_element_type=jnp.float32)[0]

def pick_rows(source, links):
    chosen = jax.vmap(lambda rows, index: rows[index])(source, jnp.clip(links, 0, N_LON - 1))
    return jnp.where((links >= 0)[:, :, None, None], chosen, jnp.zeros((), chosen.dtype))

def reference(latent, stale, stale_kv, neighbors, readers, timestep, conv_weight, time_weight, norm_gain, qkv_weight, out_weight):
    fresh_blocks = to_patches(latent)
    stale_blocks = to_patches(stale)
    bottom_rows = stale_blocks[:, :, -1]
    top_rows = stale_blocks[:, :, 0]
    from_above = jnp.concatenate([jnp.zeros_like(bottom_rows[:1]), bottom_rows[:-1]], 0)
    from_below = jnp.concatenate([top_rows[1:], jnp.zeros_like(top_rows[:1])], 0)
    north_row = pick_rows(from_above, neighbors[:, :, 0])
    south_row = pick_rows(from_below, neighbors[:, :, 1])
    stale_rows = jnp.concatenate([north_row[:, :, None], stale_blocks, south_row[:, :, None]], 2)
    fresh_rows = jnp.concatenate([north_row[:, :, None], fresh_blocks, south_row[:, :, None]], 2)
    left_column = jnp.roll(stale_rows[:, :, :, -1:], 1, axis=1)
    right_column = jnp.roll(stale_rows[:, :, :, :1], -1, axis=1)
    padded = jnp.concatenate([left_column, fresh_rows, right_column], 3)
    patch_count = N_LAT * N_LON
    tokens = LAT_CELLS * LON_CELLS
    padded = padded.reshape(patch_count, LAT_CELLS + 2, LON_CELLS + 2, CHANNELS)
    convolved = lax.conv_general_dilated(padded, conv_weight, (1, 1), 'VALID', dimension_numbers=('NHWC', 'HWIO', 'NHWC'), preferred_element_type=jnp.float32)
    lifted = convolved + time_vector(timestep, time_weight)
    fresh_flat = fresh_blocks.reshape(patch_count, LAT_CELLS, LON_CELLS, CHANNELS).astype(jnp.float32)
    mixed = (fresh_flat + jax.nn.silu(lifted)).astype(jnp.bfloat16)
    flat = mixed.reshape(-1, CHANNELS).astype(jnp.float32)
    row_mean = lax.optimization_barrier(jnp.mean(flat, axis=-1, keepdims=True))
    centered = flat - row_mean
    row_var = lax.optimization_barrier(jnp.mean(centered * centered, axis=-1, keepdims=True))
    normed = (centered * lax.rsqrt(row_var + norm_epsilon) * norm_gain).astype(jnp.bfloat16)
    projected = jnp.dot(normed, qkv_weight, preferred_element_type=jnp.float32).astype(jnp.bfloat16)
    projected = projected.reshape(patch_count, tokens, 3, HEAD_COUNT, HEAD_SIZE)
    queries = projected[:, :, 0]
    own_keys = projected[:, :, 1]
    own_values = projected[:, :, 2]
    older = stale_kv.reshape(2, N_LAT, LAT_CELLS, N_LON, LON_CELLS, HEAD_COUNT, HEAD_SIZE)
    older = older.transpose(0, 1, 3, 2, 4, 5, 6).reshape(2, N_LAT, N_LON * tokens, HEAD_COUNT, HEAD_SIZE)
    tile_index = jnp.arange(N_LON, dtype=jnp.int32)
    reads = jnp.any(readers[:, :, :, None] == tile_index[None, None, None, :], axis=2)

    def one_patch(index):
        band_index = index // N_LON
        lon_index = index % N_LON
        keys_all = jnp.concatenate([own_keys[index], older[0, band_index]], 0)
        values_all = jnp.concatenate([own_values[index], older[1, band_index]], 0)
        tile_flags = reads[band_index, :, lon_index]
        validity = jnp.concatenate([jnp.ones((tokens,), dtype=bool), jnp.repeat(tile_flags, tokens)])
        scores = jnp.einsum('qhd,khd->hqk', queries[index].astype(jnp.float32), keys_all.astype(jnp.float32)) * attention_scale
        scores = jnp.where(validity[None, None, :], scores, -1e+30)
        peak = lax.optimization_barrier(jnp.max(scores, axis=-1, keepdims=True))
        weights = jnp.exp(scores - peak)
        totals = lax.optimization_barrier(jnp.sum(weights, axis=-1))
        rounded = lax.optimization_barrier(weights.astype(jnp.bfloat16)).astype(jnp.float32)
        blended = jnp.einsum('hqk,khd->qhd', rounded, values_all.astype(jnp.float32)) / totals.T[:, :, None]
        return blended.reshape(tokens, CHANNELS).astype(jnp.bfloat16)
    attended = lax.map(one_patch, jnp.arange(patch_count, dtype=jnp.int32))
    result = flat + jnp.dot(attended.reshape(-1, CHANNELS), out_weight, preferred_element_type=jnp.float32)
    block_out = from_patches(result.astype(jnp.bfloat16).reshape(N_LAT, N_LON, LAT_CELLS, LON_CELLS, CHANNELS))
    key_whole = from_patches(own_keys.reshape(N_LAT, N_LON, LAT_CELLS, LON_CELLS, CHANNELS))
    value_whole = from_patches(own_values.reshape(N_LAT, N_LON, LAT_CELLS, LON_CELLS, CHANNELS))
    fresh_kv = jnp.stack([key_whole, value_whole], 0)
    return (block_out, fresh_kv)
```

```python
import functools
import math

import jax
import jax.numpy as jnp
from jax import lax
from jax.experimental import pallas as pl
from jax.experimental.pallas import tpu as pltpu
from jax.sharding import PartitionSpec as P

HEAD_COUNT = 10
HEAD_SIZE = 64
TIME_WIDTH = 320
LAT_CELLS, LON_CELLS, CHANNELS = 16, 32, 640
TOKENS = LAT_CELLS * LON_CELLS
N_LON, N_LAT = 32, 4
PAIRS = HEAD_COUNT // 2
POLAR = (0, 3)
INNER = (1, 2)
AXES = ("lon", "lat")
norm_epsilon = 1e-05
attention_scale = 0.125
F32, BF16 = jnp.float32, jnp.bfloat16
VMEM_LIMIT = 48 * 1024 * 1024


def time_vector(timestep, time_weight):
    half_width = TIME_WIDTH // 2
    frequency = jnp.exp(-math.log(10000.0) * jnp.arange(half_width, dtype=F32) / half_width)
    angles = timestep.astype(F32)[0] * frequency
    embedding = jnp.concatenate([jnp.cos(angles), jnp.sin(angles)])
    return jnp.dot(
        embedding[None, :], time_weight, precision=lax.Precision.HIGHEST, preferred_element_type=F32
    )


def send(value, target, bands=range(N_LAT)):
    pairs = [(p * N_LAT + b, target(p) * N_LAT + b) for p in range(N_LON) for b in bands]
    return lax.ppermute(value, AXES, pairs)


def send_band(value, moves):
    pairs = [(p * N_LAT + b, p * N_LAT + c) for p in range(N_LON) for b, c in moves]
    return lax.ppermute(value, AXES, pairs)


def partner(p):
    return p ^ 1


def ahead(p):
    return (p + (2 if p % 2 == 0 else -2)) % N_LON


def behind(p):
    return (p + (-2 if p % 2 == 0 else 2)) % N_LON


def ring_x(steps):
    return lambda p: (p - 8 * steps) % N_LON


def ring_z(steps):
    return lambda p: p // 8 * 8 + (p % 8 - 2 * steps) % 8


def tied(value, *others):
    return lax.optimization_barrier((value,) + others)[0]


def pick(flags, yes, no):
    return jnp.stack([jnp.where(flags[i], yes[i], no[i]) for i in range(2)], 0)


def dense_kernel(x_ref, w_ref, lift_ref, latent_ref, gain_ref, qkv_ref, mixed_ref, q_ref, kv_ref, acc):
    dy = pl.program_id(0)
    block = 256
    for m in range(0, TOKENS, block):
        rows = pl.ds(pl.multiple_of(dy * LON_CELLS + m, LON_CELLS), block)
        part = jnp.dot(x_ref[rows, :], w_ref[0], preferred_element_type=F32)

        @pl.when(dy == 0)
        def _(part=part, m=m):
            acc[m : m + block] = part

        @pl.when(dy > 0)
        def _(part=part, m=m):
            acc[m : m + block] += part

    @pl.when(dy == 2)
    def _():
        low = lax.broadcasted_iota(jnp.int32, (block, 128), 1) < HEAD_SIZE
        for m in range(0, TOKENS, block):
            rows = slice(m, m + block)
            lifted = acc[rows] + lift_ref[...]
            mixed = (latent_ref[rows].astype(F32) + jax.nn.silu(lifted)).astype(BF16)
            mixed_ref[rows] = mixed
            flat = mixed.astype(F32)
            mean = jnp.mean(flat, axis=-1, keepdims=True)
            centered = flat - mean
            var = jnp.mean(centered * centered, axis=-1, keepdims=True)
            normed = (centered * lax.rsqrt(var + norm_epsilon) * gain_ref[...]).astype(BF16)
            out = jnp.dot(normed, qkv_ref[...], preferred_element_type=F32)
            q = out[:, :CHANNELS].astype(BF16).astype(F32) * attention_scale
            for j in range(PAIRS):
                two = q[:, 128 * j : 128 * j + 128]
                q_ref[2 * j, rows] = jnp.where(low, two, 0.0).astype(BF16)
                q_ref[2 * j + 1, rows] = jnp.where(low, 0.0, two).astype(BF16)
            kv_ref[0, rows] = out[:, CHANNELS : 2 * CHANNELS].astype(BF16)
            kv_ref[1, rows] = out[:, 2 * CHANNELS :].astype(BF16)


def dense(x, w, lift, latent, gain, qkv):
    whole = lambda *shape: pl.BlockSpec(shape, lambda i: (0,) * len(shape))
    return pl.pallas_call(
        dense_kernel,
        grid=(3,),
        in_specs=[
            whole(18 * LON_CELLS, 3 * CHANNELS),
            pl.BlockSpec((1, 3 * CHANNELS, CHANNELS), lambda i: (i, 0, 0)),
            whole(1, CHANNELS),
            whole(TOKENS, CHANNELS),
            whole(1, CHANNELS),
            whole(CHANNELS, 3 * CHANNELS),
        ],
        out_specs=[
            whole(TOKENS, CHANNELS),
            whole(HEAD_COUNT, TOKENS, 128),
            whole(2, TOKENS, CHANNELS),
        ],
        out_shape=[
            jax.ShapeDtypeStruct((TOKENS, CHANNELS), BF16),
            jax.ShapeDtypeStruct((HEAD_COUNT, TOKENS, 128), BF16),
            jax.ShapeDtypeStruct((2, TOKENS, CHANNELS), BF16),
        ],
        scratch_shapes=[pltpu.VMEM((TOKENS, CHANNELS), F32)],
        compiler_params=pltpu.CompilerParams(vmem_limit_bytes=VMEM_LIMIT),
        cost_estimate=pl.CostEstimate(flops=5_000_000_000, bytes_accessed=16_000_000, transcendentals=400_000),
        name="dense",
    )(x, w, lift, latent, gain, qkv)


def attend_kernel(n_tiles, first, last, *refs):
    refs = list(refs)
    flags = refs.pop(0)
    q_ref = refs.pop(0)
    tiles = [(refs.pop(0), refs.pop(0)) for _ in range(n_tiles)]
    if not first:
        m_in, acc_in = refs.pop(0), refs.pop(0)
    if last:
        mixed_ref, w_ref, out_ref, m_ref, acc_ref, att_ref = refs
    else:
        m_ref, acc_ref = refs
    j = pl.program_id(0)
    if not first:
        m_ref[...] = m_in[...]
        acc_ref[...] = acc_in[...]
    block = 256
    lane = lax.broadcasted_iota(jnp.int32, (block, 128), 1)
    low = lane < HEAD_SIZE
    low_v = lax.broadcasted_iota(jnp.int32, (TOKENS, 128), 1) < HEAD_SIZE
    one_a = jnp.where(low_v, 1.0, 0.0).astype(BF16)
    one_b = jnp.where(low_v, 0.0, 1.0).astype(BF16)
    zero = jnp.zeros((TOKENS, 128), BF16)

    def one_tile(k_ref, v_ref, fresh):
        k = k_ref[0]
        v = v_ref[0]
        v_a = jnp.concatenate([jnp.where(low_v, v, zero), one_a], 1)
        v_b = jnp.concatenate([jnp.where(low_v, zero, v), one_b], 1)
        for r in range(0, TOKENS, block):
            rows = slice(r, r + block)
            nt = (((1,), (1,)), ((), ()))
            s_a = lax.dot_general(q_ref[0, rows], k, nt, preferred_element_type=F32)
            s_b = lax.dot_general(q_ref[1, rows], k, nt, preferred_element_type=F32)
            top_a = jnp.max(s_a, axis=-1, keepdims=True)
            top_b = jnp.max(s_b, axis=-1, keepdims=True)
            if not fresh:
                old = m_ref[0, rows]
                top_a = jnp.maximum(top_a, old[:, 0:1])
                top_b = jnp.maximum(top_b, old[:, 64:65])
            p_a = jnp.exp(s_a - top_a).astype(BF16)
            p_b = jnp.exp(s_b - top_b).astype(BF16)
            new = jnp.where(low, top_a, top_b)
            part = jnp.dot(p_a, v_a, preferred_element_type=F32) + jnp.dot(
                p_b, v_b, preferred_element_type=F32
            )
            if fresh:
                acc_ref[0, rows] = part
            else:
                fade = jnp.exp(old - new)
                acc_ref[0, rows] = acc_ref[0, rows] * jnp.concatenate([fade, fade], 1) + part
            m_ref[0, rows] = new

    for t, (k_ref, v_ref) in enumerate(tiles):
        if first and t == 0:
            one_tile(k_ref, v_ref, True)
        else:

            @pl.when(flags[t] != 0)
            def _(k_ref=k_ref, v_ref=v_ref):
                one_tile(k_ref, v_ref, False)

    if last:
        columns = pl.ds(pl.multiple_of(j * 128, 128), 128)
        att_ref[:, columns] = (acc_ref[0, :, :128] / acc_ref[0, :, 128:]).astype(BF16)

        @pl.when(j == PAIRS - 1)
        def _():
            for r in range(0, TOKENS, block):
                rows = slice(r, r + block)
                add = jnp.dot(att_ref[rows], w_ref[...], preferred_element_type=F32)
                out_ref[rows] = (mixed_ref[rows].astype(F32) + add).astype(BF16)


def attend(flags, q, tiles, state=None, final=None):
    first, last, n = state is None, final is not None, len(tiles)
    whole = lambda *shape: pl.BlockSpec(shape, lambda j: (0,) * len(shape))
    m_spec = pl.BlockSpec((1, TOKENS, 128), lambda j: (j, 0, 0))
    acc_spec = pl.BlockSpec((1, TOKENS, 256), lambda j: (j, 0, 0))
    in_specs = [
        pl.BlockSpec(memory_space=pltpu.SMEM),
        pl.BlockSpec((2, TOKENS, 128), lambda j: (j, 0, 0)),
    ]
    args = [flags, q]
    for tile in tiles:
        in_specs += [
            pl.BlockSpec((1, TOKENS, 128), lambda j: (0, 0, j)),
            pl.BlockSpec((1, TOKENS, 128), lambda j: (1, 0, j)),
        ]
        args += [tile, tile]
    if not first:
        in_specs += [m_spec, acc_spec]
        args += list(state)
    scratch = []
    if last:
        in_specs += [whole(TOKENS, CHANNELS), whole(CHANNELS, CHANNELS)]
        args += list(final)
        out_specs = whole(TOKENS, CHANNELS)
        out_shape = jax.ShapeDtypeStruct((TOKENS, CHANNELS), BF16)
        scratch = [
            pltpu.VMEM((1, TOKENS, 128), F32),
            pltpu.VMEM((1, TOKENS, 256), F32),
            pltpu.VMEM((TOKENS, CHANNELS), BF16),
        ]
    else:
        out_specs = [m_spec, acc_spec]
        out_shape = [
            jax.ShapeDtypeStruct((PAIRS, TOKENS, 128), F32),
            jax.ShapeDtypeStruct((PAIRS, TOKENS, 256), F32),
        ]
    return pl.pallas_call(
        functools.partial(attend_kernel, n, first, last),
        grid=(PAIRS,),
        in_specs=in_specs,
        out_specs=out_specs,
        out_shape=out_shape,
        scratch_shapes=scratch,
        compiler_params=pltpu.CompilerParams(vmem_limit_bytes=VMEM_LIMIT),
        cost_estimate=pl.CostEstimate(
            flops=n * 2_000_000_000, bytes_accessed=8_000_000, transcendentals=n * 2_600_000
        ),
        name="attend",
    )(*args)


def body(
    latent,
    stale,
    stale_kv,
    neighbors,
    readers,
    timestep,
    conv_weight,
    time_weight,
    norm_gain,
    qkv_weight,
    out_weight,
):
    band = lax.axis_index("lat")
    lon = lax.axis_index("lon")
    polar = (band == 0) | (band == N_LAT - 1)
    parity = lon % 2
    side = 1 - 2 * parity
    tile = stale_kv.reshape(2, TOKENS, CHANNELS)

    left = send(stale[:, -1:], lambda p: (p + 1) % N_LON)
    right = send(stale[:, :1], lambda p: (p - 1) % N_LON)
    tile, left, right = lax.optimization_barrier((tile, left, right))
    got_r = send(tile, partner)

    wide = jnp.stack(
        [
            jnp.concatenate([left[-1], stale[-1], right[-1]], 0),
            jnp.concatenate([left[0], stale[0], right[0]], 0),
        ],
        0,
    )
    down = jnp.minimum(band + 1, N_LAT - 1)
    up = jnp.maximum(band - 1, 0)
    shift = jnp.stack(
        [jnp.mod(neighbors[down, 0, 0], N_LON), jnp.mod(neighbors[up, 0, 1], N_LON)]
    )
    shift_x, shift_z, shift_y = shift // 8, shift // 2 % 4, shift % 2
    here_z = lon // 2 % 4
    final_y = (parity + shift_y) % 2
    carry_y = (final_y + shift_y) // 2
    final_z = jnp.mod(here_z - shift_z - carry_y, 4)
    carry_z = (final_z + shift_z + carry_y) // 4
    move_x = jnp.mod(shift_x + carry_z, 4)
    move_z = jnp.mod(shift_z + carry_y, 4)
    wide = pick(move_x % 2 == 1, send(wide, ring_x(1)), wide)
    wide = pick(move_x >= 2, send(wide, ring_x(2)), wide)
    wide = pick(move_z % 2 == 1, send(wide, ring_z(1)), wide)
    wide = pick(move_z >= 2, send(wide, ring_z(2)), wide)
    tile, wide = lax.optimization_barrier((tile, wide))
    got_f = send(tile, ahead)
    got_b = send(tile, behind)
    wide = pick(shift_y == 1, send(wide, partner), wide)
    near = send_band(jnp.where(band % 2 == 0, wide[0], wide[1]), ((0, 1), (1, 0), (2, 3), (3, 2)))
    far = send_band(jnp.where(band == 1, wide[0], wide[1]), ((1, 2), (2, 1)))
    north = jnp.where(band % 2 == 1, near, jnp.where(band == 2, far, 0))
    south = jnp.where(band % 2 == 0, near, jnp.where(band == 1, far, 0))

    middle = jnp.concatenate([left, latent, right], 1)
    padded = jnp.concatenate([north[None], middle, south[None]], 0)
    x = jnp.concatenate([padded[:, d : d + LON_CELLS] for d in range(3)], -1)
    x = x.reshape((LAT_CELLS + 2) * LON_CELLS, 3 * CHANNELS)
    lift = time_vector(timestep, time_weight)
    mixed, q, fresh = dense(
        x,
        conv_weight.reshape(3, 3 * CHANNELS, CHANNELS),
        lift,
        latent.reshape(TOKENS, CHANNELS),
        norm_gain[None, :],
        qkv_weight,
    )

    band_readers = lax.dynamic_index_in_dim(readers, band, 0, keepdims=False)
    tile_read = jnp.any(band_readers == lon, axis=-1)

    def reads(steps):
        return tile_read[jnp.mod(lon + side * steps, N_LON)]

    one = jnp.ones((1,), jnp.int32)
    flag = lambda *values: jnp.stack(values).astype(jnp.int32)

    state = attend(one, q, [fresh])
    d1_polar = send(got_r, ahead, POLAR)
    d3_a = send(got_r, behind, POLAR)
    d1_inner = send(got_b, partner, INNER)
    state = attend(flag(reads(1), reads(-2), reads(2)), q, [got_r, got_f, got_b], state)
    d3_b = send(d1_polar, ahead, POLAR)
    state = attend(
        flag(reads(-1) & polar, reads(-1) & ~polar, reads(3) & polar),
        q,
        [d1_polar, d1_inner, d3_a],
        state,
    )
    out = attend(flag(reads(-3) & polar), q, [d3_b], state, (mixed, out_weight))
    return (
        out.reshape(LAT_CELLS, LON_CELLS, CHANNELS),
        fresh.reshape(2, LAT_CELLS, LON_CELLS, CHANNELS),
    )


def solution(mesh):
    in_specs = (
        P("lat", "lon", None),
        P("lat", "lon", None),
        P(None, "lat", "lon", None),
        P(),
        P(),
        P(),
        P(),
        P(),
        P(),
        P(),
        P(),
    )
    out_specs = (P("lat", "lon", None), P(None, "lat", "lon", None))
    return jax.shard_map(body, mesh=mesh, in_specs=in_specs, out_specs=out_specs, check_vma=False)
```

```python
import functools
import math

import jax
import jax.numpy as jnp
from jax import lax
from jax.experimental import pallas as pl
from jax.experimental.pallas import tpu as pltpu
from jax.sharding import PartitionSpec as P

HEAD_COUNT = 10
HEAD_SIZE = 64
TIME_WIDTH = 320
LAT_CELLS, LON_CELLS, CHANNELS = 16, 32, 640
TOKENS = LAT_CELLS * LON_CELLS
N_LON, N_LAT = 32, 4
PAIRS = HEAD_COUNT // 2
POLAR = (0, 3)
INNER = (1, 2)
AXES = ("lon", "lat")
norm_epsilon = 1e-05
attention_scale = 0.125
F32, BF16 = jnp.float32, jnp.bfloat16
VMEM_LIMIT = 32 * 1024 * 1024


def time_vector(timestep, time_weight):
    half_width = TIME_WIDTH // 2
    frequency = jnp.exp(-math.log(10000.0) * jnp.arange(half_width, dtype=F32) / half_width)
    angles = timestep.astype(F32)[0] * frequency
    embedding = jnp.concatenate([jnp.cos(angles), jnp.sin(angles)])
    return jnp.dot(
        embedding[None, :], time_weight, precision=lax.Precision.HIGHEST, preferred_element_type=F32
    )


def send(value, target, bands=range(N_LAT)):
    pairs = [(p * N_LAT + b, target(p) * N_LAT + b) for p in range(N_LON) for b in bands]
    return lax.ppermute(value, AXES, pairs)


def send_band(value, moves):
    pairs = [(p * N_LAT + b, p * N_LAT + c) for p in range(N_LON) for b, c in moves]
    return lax.ppermute(value, AXES, pairs)


def partner(p):
    return p ^ 1


def ahead(p):
    return (p + (2 if p % 2 == 0 else -2)) % N_LON


def behind(p):
    return (p + (-2 if p % 2 == 0 else 2)) % N_LON


def ring_x(steps):
    return lambda p: (p - 8 * steps) % N_LON


def ring_z(steps):
    return lambda p: p // 8 * 8 + (p % 8 - 2 * steps) % 8


N_MASKS = 13


def setup_kernel(facts, mask_ref, flag_ref):
    lon, band = facts[0], facts[1]
    parity = lon % 2
    side = 1 - 2 * parity
    here_z = lon // 2 % 4
    polar = (band == 0) | (band == N_LAT - 1)

    def put(index, way, value):
        mask_ref[index, way] = jnp.full((1, CHANNELS), value.astype(F32), F32)

    for way in range(2):
        link = facts[2 + band * (2 * N_LON) + way]
        shift = jnp.where(link < 0, link + N_LON, link)
        shift_x, shift_z, shift_y = shift // 8, shift // 2 % 4, shift % 2
        carry_y = (parity + shift_y) // 2
        final_z = (here_z + 8 - shift_z - carry_y) % 4
        carry_z = (final_z + shift_z + carry_y) // 4
        move_x = (shift_x + carry_z) % 4
        move_z = (shift_z + carry_y) % 4
        for step in range(4):
            put(step, way, move_x == step)
            put(step + 4, way, move_z == step)
        swap = shift_y == 1
        near = (band % 2 == 1) if way == 0 else (band % 2 == 0)
        far = (band == 2) if way == 0 else (band == 1)
        put(8, way, near)
        put(9, way, far)
        put(10, way, ~swap)
        put(11, way, swap)
    put(12, 0, (band % 2) == 0)
    put(12, 1, band == 1)

    def reads(steps):
        source = (lon + side * steps + N_LON) % N_LON
        base = 2 + N_LAT * N_LON * 2 + (band * N_LON + source) * 6
        found = facts[base] == lon
        for slot in range(1, 6):
            found = found | (facts[base + slot] == lon)
        return found

    flag_ref[0] = 1
    flag_ref[1] = reads(1).astype(jnp.int32)
    flag_ref[2] = reads(-2).astype(jnp.int32)
    flag_ref[3] = reads(2).astype(jnp.int32)
    flag_ref[4] = reads(-1).astype(jnp.int32)
    flag_ref[5] = (reads(3) & polar).astype(jnp.int32)
    flag_ref[6] = (reads(-3) & polar).astype(jnp.int32)
    flag_ref[7] = polar.astype(jnp.int32)


def setup(neighbors, readers):
    smem = pl.BlockSpec(memory_space=pltpu.SMEM)
    place = jnp.stack([lax.axis_index("lon"), lax.axis_index("lat")]).astype(jnp.int32)
    facts = jnp.concatenate([place, neighbors.reshape(-1), readers.reshape(-1)])
    return pl.pallas_call(
        setup_kernel,
        in_specs=[smem],
        out_specs=[pl.BlockSpec(memory_space=pltpu.VMEM), smem],
        out_shape=[
            jax.ShapeDtypeStruct((N_MASKS, 2, 1, CHANNELS), F32),
            jax.ShapeDtypeStruct((8,), jnp.int32),
        ],
        name="setup",
    )(facts)


def conv_kernel(x_ref, w_ref, acc):
    step = pl.program_id(0)

    @pl.when(step == 0)
    def _():
        for m in range(0, TOKENS, 256):
            acc[m : m + 256] = jnp.dot(x_ref[m : m + 256], w_ref[0], preferred_element_type=F32)

    @pl.when(step == 1)
    def _():
        for m in (0, 240):
            acc[m : m + 240] += jnp.dot(
                x_ref[m + 32 : m + 272], w_ref[0], preferred_element_type=F32
            )

    @pl.when(step == 2)
    def _():
        for m in (0, 240):
            acc[m + 32 : m + 272] += jnp.dot(x_ref[m : m + 240], w_ref[0], preferred_element_type=F32)


def whole(*shape):
    return pl.BlockSpec(shape, lambda i: (0,) * len(shape))


def conv(x, w):
    return pl.pallas_call(
        conv_kernel,
        grid=(3,),
        in_specs=[
            whole(TOKENS, 3 * CHANNELS),
            pl.BlockSpec((1, 3 * CHANNELS, CHANNELS), lambda i: ((i + 1) % 3, 0, 0)),
        ],
        out_specs=whole(TOKENS, CHANNELS),
        out_shape=jax.ShapeDtypeStruct((TOKENS, CHANNELS), F32),
        compiler_params=pltpu.CompilerParams(vmem_limit_bytes=VMEM_LIMIT),
        cost_estimate=cost(1),
        name="conv",
    )(x, w)


def dense_kernel(rim_ref, w_ref, acc_ref, lift_ref, latent_ref, gain_ref, qkv_ref, mixed_ref, q_ref, kv_ref, edge):
    step = pl.program_id(0)
    rows = pl.ds(pl.multiple_of(step * LON_CELLS, LON_CELLS), LON_CELLS)
    edge[rows] = jnp.dot(rim_ref[rows], w_ref[0], preferred_element_type=F32)

    @pl.when(step == 1)
    def _():
        block = 256
        low = lax.broadcasted_iota(jnp.int32, (block, 128), 1) < HEAD_SIZE
        for m in range(0, TOKENS, block):
            rows = slice(m, m + block)
            lifted = acc_ref[rows] + lift_ref[...]
            if m == 0:
                lifted = jnp.concatenate([lifted[:LON_CELLS] + edge[:LON_CELLS], lifted[LON_CELLS:]], 0)
            else:
                lifted = jnp.concatenate([lifted[:-LON_CELLS], lifted[-LON_CELLS:] + edge[LON_CELLS:]], 0)
            mixed = (latent_ref[rows].astype(F32) + jax.nn.silu(lifted)).astype(BF16)
            mixed_ref[rows] = mixed
            flat = mixed.astype(F32)
            mean = jnp.mean(flat, axis=-1, keepdims=True)
            centered = flat - mean
            var = jnp.mean(centered * centered, axis=-1, keepdims=True)
            normed = (centered * lax.rsqrt(var + norm_epsilon) * gain_ref[...]).astype(BF16)
            out = jnp.dot(normed, qkv_ref[...], preferred_element_type=F32)
            q = out[:, :CHANNELS].astype(BF16).astype(F32) * attention_scale
            for j in range(PAIRS):
                two = q[:, 128 * j : 128 * j + 128]
                q_ref[2 * j, rows] = jnp.where(low, two, 0.0).astype(BF16)
                q_ref[2 * j + 1, rows] = jnp.where(low, 0.0, two).astype(BF16)
            kv_ref[0, rows] = out[:, CHANNELS : 2 * CHANNELS].astype(BF16)
            kv_ref[1, rows] = out[:, 2 * CHANNELS :].astype(BF16)


def dense(rims, w, acc, lift, latent, gain, qkv):
    return pl.pallas_call(
        dense_kernel,
        grid=(2,),
        in_specs=[
            whole(2 * LON_CELLS, 3 * CHANNELS),
            pl.BlockSpec((1, 3 * CHANNELS, CHANNELS), lambda i: (2 * i, 0, 0)),
            whole(TOKENS, CHANNELS),
            whole(1, CHANNELS),
            whole(TOKENS, CHANNELS),
            whole(1, CHANNELS),
            whole(CHANNELS, 3 * CHANNELS),
        ],
        out_specs=[
            whole(TOKENS, CHANNELS),
            whole(HEAD_COUNT, TOKENS, 128),
            whole(2, TOKENS, CHANNELS),
        ],
        out_shape=[
            jax.ShapeDtypeStruct((TOKENS, CHANNELS), BF16),
            jax.ShapeDtypeStruct((HEAD_COUNT, TOKENS, 128), BF16),
            jax.ShapeDtypeStruct((2, TOKENS, CHANNELS), BF16),
        ],
        scratch_shapes=[pltpu.VMEM((2 * LON_CELLS, CHANNELS), F32)],
        compiler_params=pltpu.CompilerParams(vmem_limit_bytes=VMEM_LIMIT),
        cost_estimate=cost(1),
        name="dense",
    )(rims, w, acc, lift, latent, gain, qkv)


LEAST, MOST = 1e-18, 1e18


def add_tile(flag, q_ref, k_ref, v_ref, acc_ref, fresh):
    k, v = k_ref[0], v_ref[0]
    one = jnp.ones((TOKENS, 128), BF16)
    if flag is not None:
        read = flag != 0
        k = jnp.where(read, k, jnp.zeros_like(k))
        v = jnp.where(read, v, jnp.zeros_like(v))
        one = jnp.where(read, one, jnp.zeros_like(one))
    k_t = k.T
    v_one = jnp.concatenate([v, one], 1)
    low = lax.broadcasted_iota(jnp.int32, (TOKENS, 128), 1) < HEAD_SIZE
    parts = []
    for head in range(2):
        scores = jnp.dot(q_ref[head], k_t, preferred_element_type=F32)
        parts.append(jnp.dot(jnp.exp(scores).astype(BF16), v_one, preferred_element_type=F32))
    part = jnp.concatenate(
        [
            jnp.where(low, parts[0][:, :128], parts[1][:, :128]),
            jnp.where(low, parts[0][:, 128:], parts[1][:, 128:]),
        ],
        1,
    )
    if fresh:
        acc_ref[0] = part
    else:
        acc_ref[0] += part


def attend_kernel(count, offset, first, *refs):
    refs = list(refs)
    flags, q_ref = refs.pop(0), refs.pop(0)
    tiles = [(refs.pop(0), refs.pop(0)) for _ in range(count)]
    acc_ref = refs[-1]
    if not first:
        acc_ref[...] = refs[0][...]
    for t, (k_ref, v_ref) in enumerate(tiles):
        own = first and t == 0
        add_tile(None if own else flags[offset + t], q_ref, k_ref, v_ref, acc_ref, own)


def redo_pair(j, flags, q_any, tiles, q_s, k_s, v_s, m_s, a_s, att_ref, sem):
    columns = pl.ds(pl.multiple_of(j * 128, 128), 128)
    block = 128
    low = lax.broadcasted_iota(jnp.int32, (block, 128), 1) < HEAD_SIZE

    def fetch(source, target):
        copy = pltpu.make_async_copy(source, target, sem)
        copy.start()
        copy.wait()

    fetch(q_any.at[pl.ds(2 * j, 2)], q_s)
    m_s[...] = jnp.full((TOKENS, 128), -1e30, F32)
    a_s[...] = jnp.zeros((TOKENS, 256), F32)
    for t, tile in enumerate(tiles):

        @pl.when(flags[t] != 0)
        def _(tile=tile):
            fetch(tile.at[0, :, columns], k_s)
            fetch(tile.at[1, :, columns], v_s)

            def rows_step(i, carry):
                rows = pl.ds(pl.multiple_of(i * block, block), block)
                v_one = jnp.concatenate([v_s[...], jnp.ones((TOKENS, 128), BF16)], 1)
                nt = (((1,), (1,)), ((), ()))
                old = m_s[rows]
                tops, parts = [], []
                for head in range(2):
                    scores = lax.dot_general(q_s[head, rows], k_s[...], nt, preferred_element_type=F32)
                    top = jnp.maximum(
                        jnp.max(scores, axis=-1, keepdims=True), old[:, 64 * head : 64 * head + 1]
                    )
                    p = jnp.exp(scores - top).astype(BF16)
                    tops.append(top)
                    parts.append(jnp.dot(p, v_one, preferred_element_type=F32))
                new = jnp.where(low, tops[0], tops[1])
                fade = jnp.exp(old - new)
                part = jnp.concatenate(
                    [
                        jnp.where(low, parts[0][:, :128], parts[1][:, :128]),
                        jnp.where(low, parts[0][:, 128:], parts[1][:, 128:]),
                    ],
                    1,
                )
                a_s[rows] = a_s[rows] * jnp.concatenate([fade, fade], 1) + part
                m_s[rows] = new
                return carry

            lax.fori_loop(0, TOKENS // block, rows_step, 0)

    att_ref[:, columns] = (a_s[:, :128] / a_s[:, 128:]).astype(BF16)


def finish_kernel(count, offset, total, *refs):
    refs = list(refs)
    flags, q_ref = refs.pop(0), refs.pop(0)
    tiles = [(refs.pop(0), refs.pop(0)) for _ in range(count)]
    acc_in, mixed_ref, w_ref, q_any = refs[:4]
    every = refs[4 : 4 + total]
    out_ref, acc_ref, att_ref, bad, q_s, k_s, v_s, m_s, a_s, sem = refs[4 + total :]
    j = pl.program_id(0)
    acc_ref[...] = acc_in[...]
    for t, (k_ref, v_ref) in enumerate(tiles):
        add_tile(flags[offset + t], q_ref, k_ref, v_ref, acc_ref, False)
    columns = pl.ds(pl.multiple_of(j * 128, 128), 128)
    totals = acc_ref[0, :, 128:]
    att_ref[:, columns] = (acc_ref[0, :, :128] / totals).astype(BF16)
    fine = (jnp.min(totals) > LEAST) & (jnp.max(totals) < MOST)
    bad[0] = jnp.where(j == 0, 0, bad[0]) + jnp.where(fine, 0, 1)

    @pl.when(j == PAIRS - 1)
    def _():
        @pl.when(bad[0] != 0)
        def _():
            def one_pair(i, carry):
                redo_pair(i, flags, q_any, every, q_s, k_s, v_s, m_s, a_s, att_ref, sem)
                return carry

            lax.fori_loop(0, PAIRS, one_pair, 0)

        for r in range(0, TOKENS, 256):
            rows = slice(r, r + 256)
            add = jnp.dot(att_ref[rows], w_ref[...], preferred_element_type=F32)
            out_ref[rows] = (mixed_ref[rows].astype(F32) + add).astype(BF16)


ACC_SPEC = pl.BlockSpec((1, TOKENS, 256), lambda j: (j, 0, 0))
ACC_SHAPE = jax.ShapeDtypeStruct((PAIRS, TOKENS, 256), F32)


def tile_specs(flags, q, tiles):
    specs = [
        pl.BlockSpec(memory_space=pltpu.SMEM),
        pl.BlockSpec((2, TOKENS, 128), lambda j: (j, 0, 0)),
    ]
    args = [flags, q]
    for tile in tiles:
        specs += [
            pl.BlockSpec((1, TOKENS, 128), lambda j: (0, 0, j)),
            pl.BlockSpec((1, TOKENS, 128), lambda j: (1, 0, j)),
        ]
        args += [tile, tile]
    return specs, args


def cost(n):
    return pl.CostEstimate(flops=n * 4_600_000_000, bytes_accessed=1_000_000, transcendentals=0)


def attend(flags, q, tiles, offset, acc=None):
    specs, args = tile_specs(flags, q, tiles)
    if acc is not None:
        specs.append(ACC_SPEC)
        args.append(acc)
    return pl.pallas_call(
        functools.partial(attend_kernel, len(tiles), offset, acc is None),
        grid=(PAIRS,),
        in_specs=specs,
        out_specs=ACC_SPEC,
        out_shape=ACC_SHAPE,
        compiler_params=pltpu.CompilerParams(vmem_limit_bytes=VMEM_LIMIT),
        cost_estimate=cost(len(tiles)),
        name="attend",
    )(*args)


def finish(flags, q, tiles, offset, acc, mixed, out_weight, every):
    specs, args = tile_specs(flags, q, tiles)
    anywhere = pl.BlockSpec(memory_space=pl.ANY)
    specs += [ACC_SPEC, whole(TOKENS, CHANNELS), whole(CHANNELS, CHANNELS)] + [anywhere] * (1 + len(every))
    args += [acc, mixed, out_weight, q] + every
    return pl.pallas_call(
        functools.partial(finish_kernel, len(tiles), offset, len(every)),
        grid=(PAIRS,),
        in_specs=specs,
        out_specs=whole(TOKENS, CHANNELS),
        out_shape=jax.ShapeDtypeStruct((TOKENS, CHANNELS), BF16),
        scratch_shapes=[
            pltpu.VMEM((1, TOKENS, 256), F32),
            pltpu.VMEM((TOKENS, CHANNELS), BF16),
            pltpu.SMEM((1,), jnp.int32),
            pltpu.VMEM((2, TOKENS, 128), BF16),
            pltpu.VMEM((TOKENS, 128), BF16),
            pltpu.VMEM((TOKENS, 128), BF16),
            pltpu.VMEM((TOKENS, 128), F32),
            pltpu.VMEM((TOKENS, 256), F32),
            pltpu.SemaphoreType.DMA,
        ],
        compiler_params=pltpu.CompilerParams(vmem_limit_bytes=VMEM_LIMIT),
        cost_estimate=cost(len(tiles)),
        name="finish",
    )(*args)


def body(
    latent,
    stale,
    stale_kv,
    neighbors,
    readers,
    timestep,
    conv_weight,
    time_weight,
    norm_gain,
    qkv_weight,
    out_weight,
):
    tile = stale_kv.reshape(2, TOKENS, CHANNELS)
    weights = conv_weight.reshape(3, 3 * CHANNELS, CHANNELS)

    left = send(stale[:, -1:], lambda p: (p + 1) % N_LON)
    right = send(stale[:, :1], lambda p: (p - 1) % N_LON)
    tile, left, right, neighbors, readers = lax.optimization_barrier(
        (tile, left, right, neighbors, readers)
    )
    masks, flags = setup(neighbors, readers)
    got_f = send(tile, ahead)
    got_b = send(tile, behind)

    wide = jnp.stack(
        [
            jnp.concatenate([left[-1], stale[-1], right[-1]], 0),
            jnp.concatenate([left[0], stale[0], right[0]], 0),
        ],
        0,
    )
    def shifted(rows):
        x = jnp.concatenate([rows[:, d : d + LON_CELLS] for d in range(3)], -1)
        return x.reshape(-1, 3 * CHANNELS)

    acc = conv(shifted(jnp.concatenate([left, latent, right], 1)), weights)
    def choose(moved, base):
        total = moved[0].astype(F32) * masks[base]
        for step in range(1, len(moved)):
            total += moved[step].astype(F32) * masks[base + step]
        return total.astype(BF16)

    def either(which):
        part = masks[12, which]
        return (wide[0].astype(F32) * part + wide[1].astype(F32) * (1 - part)).astype(BF16)

    near_row = either(0)
    far_row = either(1)
    near, far = ((0, 1), (1, 0), (2, 3), (3, 2)), ((1, 2), (2, 1))
    moved = [send_band(near_row, near), send_band(far_row, far)]
    wide = choose(moved, 8)
    wide = choose([wide, send(wide, partner)], 10)
    late, wide = lax.optimization_barrier((tile, wide))
    got_r = send(late, partner)
    got_f, got_b, wide, acc = lax.optimization_barrier((got_f, got_b, wide, acc))
    wide = choose([wide] + [send(wide, ring_x(s)) for s in (1, 2, 3)], 0)
    wide = choose([wide] + [send(wide, ring_z(s)) for s in (1, 2, 3)], 4)

    lift = time_vector(timestep, time_weight)
    mixed, q, fresh = dense(
        shifted(wide),
        weights,
        acc,
        lift,
        latent.reshape(TOKENS, CHANNELS),
        norm_gain[None, :],
        qkv_weight,
    )

    d1_polar = send(lax.optimization_barrier((got_r, got_f))[0], ahead, POLAR)
    d3_a = send(lax.optimization_barrier((got_r, got_b))[0], behind, POLAR)
    d1_inner = send(lax.optimization_barrier((got_b, got_r))[0], partner, INNER)
    sums = attend(flags, q, [fresh, got_r], 0)
    sums = attend(flags, q, [got_f, got_b], 2, sums)
    d3_b = send(d1_polar, ahead, POLAR)
    d1 = jnp.where(flags[7] != 0, d1_polar, d1_inner)
    sums = attend(flags, q, [d1, d3_a], 4, sums)
    every = [fresh, got_r, got_f, got_b, d1, d3_a, d3_b]
    out = finish(flags, q, [d3_b], 6, sums, mixed, out_weight, every)
    return (
        out.reshape(LAT_CELLS, LON_CELLS, CHANNELS),
        fresh.reshape(2, LAT_CELLS, LON_CELLS, CHANNELS),
    )


def solution(mesh):
    in_specs = (
        P("lat", "lon", None),
        P("lat", "lon", None),
        P(None, "lat", "lon", None),
        P(),
        P(),
        P(),
        P(),
        P(),
        P(),
        P(),
        P(),
    )
    out_specs = (P("lat", "lon", None), P(None, "lat", "lon", None))
    return jax.shard_map(body, mesh=mesh, in_specs=in_specs, out_specs=out_specs, check_vma=False)
```

```python
import functools
import math

import jax
import jax.numpy as jnp
from jax import lax
from jax.experimental import pallas as pl
from jax.experimental.pallas import tpu as pltpu
from jax.sharding import PartitionSpec as P

HEAD_COUNT = 10
HEAD_SIZE = 64
TIME_WIDTH = 320
LAT_CELLS, LON_CELLS, CHANNELS = 16, 32, 640
TOKENS = LAT_CELLS * LON_CELLS
N_LON, N_LAT = 32, 4
PAIRS = HEAD_COUNT // 2
POLAR = (0, 3)
INNER = (1, 2)
AXES = ("lon", "lat")
norm_epsilon = 1e-05
attention_scale = 0.125
F32, BF16 = jnp.float32, jnp.bfloat16
VMEM_LIMIT = 32 * 1024 * 1024


def time_vector(timestep, time_weight):
    half_width = TIME_WIDTH // 2
    frequency = jnp.exp(-math.log(10000.0) * jnp.arange(half_width, dtype=F32) / half_width)
    angles = timestep.astype(F32)[0] * frequency
    embedding = jnp.concatenate([jnp.cos(angles), jnp.sin(angles)])
    return jnp.dot(
        embedding[None, :], time_weight, precision=lax.Precision.HIGHEST, preferred_element_type=F32
    )


def send(value, target, bands=range(N_LAT)):
    pairs = [(p * N_LAT + b, target(p, b) * N_LAT + b) for p in range(N_LON) for b in bands]
    return lax.ppermute(value, AXES, pairs)


def send_band(value, moves):
    pairs = [(p * N_LAT + b, p * N_LAT + c) for p in range(N_LON) for b, c in moves]
    return lax.ppermute(value, AXES, pairs)


def partner(p, band=0):
    return p ^ 1


def aside(p, band=0):
    return (p + (-1 if p % 2 == 0 else 1)) % N_LON


def ahead(p, band=0):
    return (p + (2 if p % 2 == 0 else -2)) % N_LON


def behind(p, band=0):
    return (p + (-2 if p % 2 == 0 else 2)) % N_LON


def ring_x(steps):
    return lambda p, band: (p - 8 * steps) % N_LON


def ring_z(steps):
    return lambda p, band: p // 8 * 8 + (p % 8 - 2 * steps) % 8


N_MASKS = 28
X_MASKS, Z_MASKS, Y_MASKS, NEAR, FAR = 0, 8, 16, 20, 24


def prepare_kernel(place, links_ref, left_ref, right_ref, top_ref, low_ref, mask_ref, wide_ref):
    lon, band = place[0], place[1]
    parity, here_z = lon % 2, lon // 2 % 4

    def put(at, value):
        mask_ref[at : at + 1] = jnp.broadcast_to(value.astype(F32), (1, CHANNELS))

    for way in range(2):
        target = jnp.minimum(band + 1, N_LAT - 1) if way == 0 else jnp.maximum(band - 1, 0)
        links = links_ref[target]
        link = jnp.broadcast_to(links[0:1, way : way + 1], (1, CHANNELS))
        shift = jnp.where(link < 0, link + N_LON, link)
        shift_x, shift_z, shift_y = shift >> 3, (shift >> 1) & 3, shift & 1
        carry_y = (((parity + shift_y) & 1) + shift_y) >> 1
        final_z = (here_z + 8 - shift_z - carry_y) & 3
        carry_z = (final_z + shift_z + carry_y) >> 2
        move_x = (shift_x + carry_z) & 3
        move_z = (shift_z + carry_y) & 3
        for step in range(4):
            put(X_MASKS + 2 * step + way, move_x == step)
            put(Z_MASKS + 2 * step + way, move_z == step)
        own = jnp.broadcast_to(links_ref[band][0:1, way : way + 1], (1, CHANNELS))
        for step in range(2):
            put(Y_MASKS + 2 * step + way, (own & 1) == step)
    flat = lambda value: jnp.full((1, CHANNELS), value.astype(F32), F32)
    put(NEAR, flat(band % 2 == 0))
    put(NEAR + 1, flat(band % 2 == 1))
    put(NEAR + 2, flat(band % 2 == 1))
    put(NEAR + 3, flat(band % 2 == 0))
    put(FAR, flat(band == 1))
    put(FAR + 1, flat(band == 2))
    put(FAR + 2, flat(band == 2))
    put(FAR + 3, flat(band == 1))
    for way, (row_ref, at) in enumerate(((low_ref, LAT_CELLS - 1), (top_ref, 0))):
        wide_ref[way, 0:LON_CELLS] = row_ref[0]
        corners = [ref[at].astype(F32) for ref in (left_ref, right_ref)]
        wide_ref[way, LON_CELLS : LON_CELLS + 2] = jnp.concatenate(corners, 0).astype(BF16)


def prepare(place, neighbors, left, right, stale):
    row = lambda at: pl.BlockSpec((1, LON_CELLS, CHANNELS), lambda i: (at, 0, 0))
    return pl.pallas_call(
        prepare_kernel,
        grid=(1,),
        in_specs=[
            pl.BlockSpec(memory_space=pltpu.SMEM),
            whole(N_LAT, N_LON, 2),
            whole(LAT_CELLS, 1, CHANNELS),
            whole(LAT_CELLS, 1, CHANNELS),
            row(0),
            row(LAT_CELLS - 1),
        ],
        out_specs=[whole(N_MASKS, CHANNELS), whole(2, LON_CELLS + 2, CHANNELS)],
        out_shape=[
            jax.ShapeDtypeStruct((N_MASKS, CHANNELS), F32),
            jax.ShapeDtypeStruct((2, LON_CELLS + 2, CHANNELS), BF16),
        ],
        name="prepare",
    )(place, neighbors, left, right, stale, stale)


def flags_kernel(place, readers_ref, flag_ref):
    lon, band = place[0], place[1]
    side = 1 - 2 * (lon % 2)
    polar = (band == 0) | (band == N_LAT - 1)
    hit = (readers_ref[band] == lon).astype(jnp.int32)
    row = lax.broadcasted_iota(jnp.int32, hit.shape, 0)

    def reads(steps):
        source = (lon + side * steps + N_LON) % N_LON
        return jnp.max(jnp.where(row == source, hit, 0))

    only_polar = polar.astype(jnp.int32)
    flag_ref[0] = 1
    flag_ref[1] = reads(1)
    flag_ref[2] = reads(-2)
    flag_ref[3] = reads(2)
    flag_ref[4] = reads(-1) * only_polar
    flag_ref[5] = reads(3) * only_polar
    flag_ref[6] = jnp.where(polar, reads(-3), reads(-1))
    flag_ref[7] = only_polar


def flags_of(place, readers):
    smem = pl.BlockSpec(memory_space=pltpu.SMEM)
    return pl.pallas_call(
        flags_kernel,
        in_specs=[smem, pl.BlockSpec(memory_space=pltpu.VMEM)],
        out_specs=smem,
        out_shape=jax.ShapeDtypeStruct((8,), jnp.int32),
        name="flags",
    )(place, readers)


def conv_kernel(x_ref, w_ref, acc):
    step = pl.program_id(0)

    @pl.when(step == 0)
    def _():
        for m in range(0, TOKENS, 256):
            acc[m : m + 256] = jnp.dot(x_ref[m : m + 256], w_ref[0], preferred_element_type=F32)

    @pl.when(step == 1)
    def _():
        for m in (0, 240):
            acc[m : m + 240] += jnp.dot(
                x_ref[m + 32 : m + 272], w_ref[0], preferred_element_type=F32
            )

    @pl.when(step == 2)
    def _():
        for m in (0, 240):
            acc[m + 32 : m + 272] += jnp.dot(x_ref[m : m + 240], w_ref[0], preferred_element_type=F32)


def whole(*shape):
    return pl.BlockSpec(shape, lambda i: (0,) * len(shape))


def conv(x, w):
    return pl.pallas_call(
        conv_kernel,
        grid=(3,),
        in_specs=[
            whole(TOKENS, 3 * CHANNELS),
            pl.BlockSpec((1, 3 * CHANNELS, CHANNELS), lambda i: ((i + 1) % 3, 0, 0)),
        ],
        out_specs=whole(TOKENS, CHANNELS),
        out_shape=jax.ShapeDtypeStruct((TOKENS, CHANNELS), F32),
        compiler_params=pltpu.CompilerParams(vmem_limit_bytes=VMEM_LIMIT),
        cost_estimate=cost(1),
        name="conv",
    )(x, w)


def dense_kernel(
    rim_ref,
    lift_ref,
    gain_ref,
    w_any,
    acc_any,
    latent_any,
    qkv_any,
    mixed_ref,
    q_ref,
    kv_ref,
    acc_ref,
    latent_ref,
    qkv_ref,
    w_ref,
    sems,
):
    moves = [(acc_any, acc_ref), (latent_any, latent_ref), (qkv_any, qkv_ref)]
    moves += [(w_any.at[0], w_ref.at[0]), (w_any.at[2], w_ref.at[1])]
    copies = [pltpu.make_async_copy(a, b, sems.at[i]) for i, (a, b) in enumerate(moves)]
    for copy in copies:
        copy.start()
    block = 128
    low = lax.broadcasted_iota(jnp.int32, (block, 128), 1) < HEAD_SIZE

    def rows_of(m):
        rows = slice(m, m + block)
        lifted = acc_ref[rows] + lift_ref[...]
        if m == 0:
            copies[3].wait()
            edge = jnp.dot(rim_ref[:LON_CELLS], w_ref[0], preferred_element_type=F32)
            lifted = jnp.concatenate([lifted[:LON_CELLS] + edge, lifted[LON_CELLS:]], 0)
        if m == TOKENS - block:
            copies[4].wait()
            edge = jnp.dot(rim_ref[LON_CELLS:], w_ref[1], preferred_element_type=F32)
            lifted = jnp.concatenate([lifted[:-LON_CELLS], lifted[-LON_CELLS:] + edge], 0)
        mixed = (latent_ref[rows].astype(F32) + jax.nn.silu(lifted)).astype(BF16)
        mixed_ref[rows] = mixed
        flat = mixed.astype(F32)
        mean = jnp.mean(flat, axis=-1, keepdims=True)
        centered = flat - mean
        var = jnp.mean(centered * centered, axis=-1, keepdims=True)
        normed = (centered * lax.rsqrt(var + norm_epsilon) * gain_ref[...]).astype(BF16)
        if m == block:
            copies[2].wait()
        out = jnp.dot(normed, qkv_ref[...], preferred_element_type=F32)
        q = out[:, :CHANNELS].astype(BF16).astype(F32) * attention_scale
        for j in range(PAIRS):
            two = q[:, 128 * j : 128 * j + 128]
            q_ref[2 * j, rows] = jnp.where(low, two, 0.0).astype(BF16)
            q_ref[2 * j + 1, rows] = jnp.where(low, 0.0, two).astype(BF16)
        for i in range(2):
            part = out[:, (i + 1) * CHANNELS : (i + 2) * CHANNELS].astype(BF16)
            kv_ref[i, rows] = part

    copies[0].wait()
    copies[1].wait()
    for m in (block, 2 * block, 0, 3 * block):
        rows_of(m)


def dense(rims, w, acc, lift, latent, gain, qkv):
    vmem, anywhere = pl.BlockSpec(memory_space=pltpu.VMEM), pl.BlockSpec(memory_space=pl.ANY)
    return pl.pallas_call(
        dense_kernel,
        in_specs=[vmem] * 3 + [anywhere] * 4,
        out_specs=[vmem] * 3,
        out_shape=[
            jax.ShapeDtypeStruct((TOKENS, CHANNELS), BF16),
            jax.ShapeDtypeStruct((HEAD_COUNT, TOKENS, 128), BF16),
            jax.ShapeDtypeStruct((2, TOKENS, CHANNELS), BF16),
        ],
        scratch_shapes=[
            pltpu.VMEM((TOKENS, CHANNELS), F32),
            pltpu.VMEM((TOKENS, CHANNELS), BF16),
            pltpu.VMEM((CHANNELS, 3 * CHANNELS), BF16),
            pltpu.VMEM((2, 3 * CHANNELS, CHANNELS), BF16),
            pltpu.SemaphoreType.DMA((5,)),
        ],
        compiler_params=pltpu.CompilerParams(vmem_limit_bytes=54 * 1024 * 1024),
        cost_estimate=cost(0.01),
        name="dense",
    )(rims, lift, gain, w, acc, latent, qkv)


LEAST, MOST = 1e-18, 1e18


def add_tile(flag, q_ref, k_ref, v_ref, acc_ref, fresh):
    k, v = k_ref[0], v_ref[0]
    one = jnp.ones((TOKENS, 128), BF16)
    if flag is not None:
        read = flag != 0
        k = jnp.where(read, k, jnp.zeros_like(k))
        v = jnp.where(read, v, jnp.zeros_like(v))
        one = jnp.where(read, one, jnp.zeros_like(one))
    k_t = k.T
    v_one = jnp.concatenate([v, one], 1)
    low = lax.broadcasted_iota(jnp.int32, (TOKENS, 128), 1) < HEAD_SIZE
    parts = []
    for head in range(2):
        scores = jnp.dot(q_ref[head], k_t, preferred_element_type=F32)
        parts.append(jnp.dot(jnp.exp(scores).astype(BF16), v_one, preferred_element_type=F32))
    part = jnp.concatenate(
        [
            jnp.where(low, parts[0][:, :128], parts[1][:, :128]),
            jnp.where(low, parts[0][:, 128:], parts[1][:, 128:]),
        ],
        1,
    )
    if fresh:
        acc_ref[0] = part
    else:
        acc_ref[0] += part


def attend_kernel(count, offset, first, *refs):
    refs = list(refs)
    flags, q_ref = refs.pop(0), refs.pop(0)
    tiles = [(refs.pop(0), refs.pop(0)) for _ in range(count)]
    acc_ref = refs[-1]
    if not first:
        acc_ref[...] = refs[0][...]
    for t, (k_ref, v_ref) in enumerate(tiles):
        own = first and t == 0
        add_tile(None if own else flags[offset + t], q_ref, k_ref, v_ref, acc_ref, own)


def redo_pair(j, flags, q_any, tiles, q_s, k_s, v_s, m_s, a_s, att_ref, sem):
    columns = pl.ds(pl.multiple_of(j * 128, 128), 128)
    block = 128
    low = lax.broadcasted_iota(jnp.int32, (block, 128), 1) < HEAD_SIZE

    def fetch(source, target):
        copy = pltpu.make_async_copy(source, target, sem)
        copy.start()
        copy.wait()

    fetch(q_any.at[pl.ds(2 * j, 2)], q_s)
    m_s[...] = jnp.full((TOKENS, 128), -1e30, F32)
    a_s[...] = jnp.zeros((TOKENS, 256), F32)
    for t, tile in enumerate(tiles):

        @pl.when(flags[t] != 0)
        def _(tile=tile):
            k_any, k_at, v_any, v_at = tile
            fetch(k_any.at[k_at, :, columns], k_s)
            fetch(v_any.at[v_at, :, columns], v_s)

            def rows_step(i, carry):
                rows = pl.ds(pl.multiple_of(i * block, block), block)
                v_one = jnp.concatenate([v_s[...], jnp.ones((TOKENS, 128), BF16)], 1)
                nt = (((1,), (1,)), ((), ()))
                old = m_s[rows]
                tops, parts = [], []
                for head in range(2):
                    scores = lax.dot_general(q_s[head, rows], k_s[...], nt, preferred_element_type=F32)
                    top = jnp.maximum(
                        jnp.max(scores, axis=-1, keepdims=True), old[:, 64 * head : 64 * head + 1]
                    )
                    p = jnp.exp(scores - top).astype(BF16)
                    tops.append(top)
                    parts.append(jnp.dot(p, v_one, preferred_element_type=F32))
                new = jnp.where(low, tops[0], tops[1])
                fade = jnp.exp(old - new)
                part = jnp.concatenate(
                    [
                        jnp.where(low, parts[0][:, :128], parts[1][:, :128]),
                        jnp.where(low, parts[0][:, 128:], parts[1][:, 128:]),
                    ],
                    1,
                )
                a_s[rows] = a_s[rows] * jnp.concatenate([fade, fade], 1) + part
                m_s[rows] = new
                return carry

            lax.fori_loop(0, TOKENS // block, rows_step, 0)

    att_ref[:, columns] = (a_s[:, :128] / a_s[:, 128:]).astype(BF16)


def finish_kernel(count, offset, places, *refs):
    refs = list(refs)
    flags, q_ref = refs.pop(0), refs.pop(0)
    tiles = [(refs.pop(0), refs.pop(0)) for _ in range(count)]
    acc_in, mixed_ref, w_ref, q_any = refs[:4]
    every = [(refs[4 + k], k_at, refs[4 + v], v_at) for k, k_at, v, v_at in places]
    out_ref, acc_ref, att_ref, bad, q_s, k_s, v_s, m_s, a_s, sem = refs[-10:]
    j = pl.program_id(0)
    acc_ref[...] = acc_in[...]
    for t, (k_ref, v_ref) in enumerate(tiles):
        add_tile(flags[offset + t], q_ref, k_ref, v_ref, acc_ref, False)
    columns = pl.ds(pl.multiple_of(j * 128, 128), 128)
    totals = acc_ref[0, :, 128:]
    att_ref[:, columns] = (acc_ref[0, :, :128] / totals).astype(BF16)
    fine = (jnp.min(totals) > LEAST) & (jnp.max(totals) < MOST)
    bad[0] = jnp.where(j == 0, 0, bad[0]) + jnp.where(fine, 0, 1)

    @pl.when(j == PAIRS - 1)
    def _():
        @pl.when(bad[0] != 0)
        def _():
            def one_pair(i, carry):
                redo_pair(i, flags, q_any, every, q_s, k_s, v_s, m_s, a_s, att_ref, sem)
                return carry

            lax.fori_loop(0, PAIRS, one_pair, 0)

        for r in range(0, TOKENS, 256):
            rows = slice(r, r + 256)
            add = jnp.dot(att_ref[rows], w_ref[...], preferred_element_type=F32)
            out_ref[rows] = (mixed_ref[rows].astype(F32) + add).astype(BF16)


ACC_SPEC = pl.BlockSpec((1, TOKENS, 256), lambda j: (j, 0, 0))
ACC_SHAPE = jax.ShapeDtypeStruct((PAIRS, TOKENS, 256), F32)


def tile_specs(flags, q, tiles):
    specs = [
        pl.BlockSpec(memory_space=pltpu.SMEM),
        pl.BlockSpec((2, TOKENS, 128), lambda j: (j, 0, 0)),
    ]
    args = [flags, q]
    for k, k_at, v, v_at in tiles:
        specs += [
            pl.BlockSpec((1, TOKENS, 128), lambda j, at=k_at: (at, 0, j)),
            pl.BlockSpec((1, TOKENS, 128), lambda j, at=v_at: (at, 0, j)),
        ]
        args += [k, v]
    return specs, args


def one(tile):
    return tile, 0, tile, 1


def cost(n):
    return pl.CostEstimate(flops=int(n * 4_600_000_000), bytes_accessed=1_000_000, transcendentals=0)


def attend(flags, q, tiles, offset, acc=None):
    specs, args = tile_specs(flags, q, tiles)
    if acc is not None:
        specs.append(ACC_SPEC)
        args.append(acc)
    return pl.pallas_call(
        functools.partial(attend_kernel, len(tiles), offset, acc is None),
        grid=(PAIRS,),
        in_specs=specs,
        out_specs=ACC_SPEC,
        out_shape=ACC_SHAPE,
        compiler_params=pltpu.CompilerParams(vmem_limit_bytes=20 * 1024 * 1024),
        cost_estimate=cost(0.01),
        name="attend",
    )(*args)


def finish(flags, q, tiles, offset, acc, mixed, out_weight, every):
    specs, args = tile_specs(flags, q, tiles)
    anywhere = pl.BlockSpec(memory_space=pl.ANY)
    arrays, places = [], []
    for k, k_at, v, v_at in every:
        where = []
        for array in (k, v):
            known = [i for i, other in enumerate(arrays) if other is array]
            if not known:
                arrays.append(array)
            where.append(known[0] if known else len(arrays) - 1)
        places.append((where[0], k_at, where[1], v_at))
    specs += [ACC_SPEC, whole(TOKENS, CHANNELS), whole(CHANNELS, CHANNELS)]
    specs += [anywhere] * (1 + len(arrays))
    args += [acc, mixed, out_weight, q] + arrays
    return pl.pallas_call(
        functools.partial(finish_kernel, len(tiles), offset, tuple(places)),
        grid=(PAIRS,),
        in_specs=specs,
        out_specs=whole(TOKENS, CHANNELS),
        out_shape=jax.ShapeDtypeStruct((TOKENS, CHANNELS), BF16),
        scratch_shapes=[
            pltpu.VMEM((1, TOKENS, 256), F32),
            pltpu.VMEM((TOKENS, CHANNELS), BF16),
            pltpu.SMEM((1,), jnp.int32),
            pltpu.VMEM((2, TOKENS, 128), BF16),
            pltpu.VMEM((TOKENS, 128), BF16),
            pltpu.VMEM((TOKENS, 128), BF16),
            pltpu.VMEM((TOKENS, 128), F32),
            pltpu.VMEM((TOKENS, 256), F32),
            pltpu.SemaphoreType.DMA,
        ],
        compiler_params=pltpu.CompilerParams(vmem_limit_bytes=20 * 1024 * 1024),
        cost_estimate=cost(len(tiles)),
        name="finish",
    )(*args)


def body(
    latent,
    stale,
    stale_kv,
    neighbors,
    readers,
    timestep,
    conv_weight,
    time_weight,
    norm_gain,
    qkv_weight,
    out_weight,
):
    tile = stale_kv.reshape(2, TOKENS, CHANNELS)
    weights = conv_weight.reshape(3, 3 * CHANNELS, CHANNELS)
    place = jnp.stack([lax.axis_index("lon"), lax.axis_index("lat")]).astype(jnp.int32)

    left = send(stale[:, -1:], lambda p, band: (p + 1) % N_LON)
    right = send(stale[:, :1], lambda p, band: (p - 1) % N_LON)

    tile, left, right = lax.optimization_barrier((tile, left, right))
    got_r = send(tile, partner)

    masks, wide = prepare(place, neighbors, left, right, stale)

    def choose(moved, base):
        rows = []
        for way in range(2):
            total = moved[0][way].astype(F32) * masks[base + way]
            for step in range(1, len(moved)):
                total += moved[step][way].astype(F32) * masks[base + 2 * step + way]
            rows.append(total.astype(BF16))
        return jnp.stack(rows, 0)

    def shifted(rows):
        x = jnp.concatenate([rows[:, d : d + LON_CELLS] for d in range(3)], -1)
        return x.reshape(-1, 3 * CHANNELS)

    wide = choose([wide] + [send(wide, ring_x(s)) for s in (1, 2, 3)], X_MASKS)
    wide = choose([wide] + [send(wide, ring_z(s)) for s in (1, 2, 3)], Z_MASKS)
    tile, wide, latent, readers, timestep, norm_gain = lax.optimization_barrier(
        (tile, wide, latent, readers, timestep, norm_gain[None, :])
    )
    got_f = send(tile, ahead)
    got_b = send(tile, behind)
    acc = conv(shifted(jnp.concatenate([left, latent, right], 1)), weights)
    lift = time_vector(timestep, time_weight)
    flags = flags_of(place, readers)

    wide, acc, got_r, lift, flags = lax.optimization_barrier((wide, acc, got_r, lift, flags))
    both = lambda base: (wide[0].astype(F32) * masks[base] + wide[1].astype(F32) * masks[base + 1]).astype(BF16)
    near = send_band(both(NEAR), ((0, 1), (1, 0), (2, 3), (3, 2)))
    far = send_band(both(FAR), ((1, 2), (2, 1)))
    near, far = near.astype(F32), far.astype(F32)
    wide = jnp.stack(
        [(near * masks[NEAR + 2 + i] + far * masks[FAR + 2 + i]).astype(BF16) for i in range(2)], 0
    )
    swapped = send(wide, partner)
    wide = choose([wide, swapped], Y_MASKS)

    rims = jnp.concatenate([wide[:, LON_CELLS : LON_CELLS + 1], wide[:, :LON_CELLS], wide[:, LON_CELLS + 1 :]], 1)
    mixed, q, fresh = dense(
        shifted(rims),
        weights,
        acc,
        lift,
        latent.reshape(TOKENS, CHANNELS),
        norm_gain,
        qkv_weight,
    )

    got_t = send(got_r, ahead, POLAR)
    got_u = send(got_r, behind, POLAR)
    got_b, got_f, q = lax.optimization_barrier((got_b, got_f, q))
    got_s = send(got_b, lambda p, band: aside(p) if band in POLAR else partner(p))
    sums = attend(flags, q, [one(fresh), one(got_r)], 0)
    sums = attend(flags, q, [one(got_f), one(got_b)], 2, sums)
    sums = attend(flags, q, [one(got_t), one(got_u)], 4, sums)
    every = [one(tile) for tile in (fresh, got_r, got_f, got_b, got_t, got_u, got_s)]
    out = finish(flags, q, [one(got_s)], 6, sums, mixed, out_weight, every)
    return (
        out.reshape(LAT_CELLS, LON_CELLS, CHANNELS),
        fresh.reshape(2, LAT_CELLS, LON_CELLS, CHANNELS),
    )


def solution(mesh):
    in_specs = (
        P("lat", "lon", None),
        P("lat", "lon", None),
        P(None, "lat", "lon", None),
        P(),
        P(),
        P(),
        P(),
        P(),
        P(),
        P(),
        P(),
    )
    out_specs = (P("lat", "lon", None), P(None, "lat", "lon", None))
    return jax.shard_map(body, mesh=mesh, in_specs=in_specs, out_specs=out_specs, check_vma=False)
```

```python
import functools
import math

import jax
import jax.numpy as jnp
from jax import lax
from jax.experimental import pallas as pl
from jax.experimental.pallas import tpu as pltpu
from jax.sharding import PartitionSpec as P

HEAD_COUNT = 10
HEAD_SIZE = 64
TIME_WIDTH = 320
LAT_CELLS, LON_CELLS, CHANNELS = 16, 32, 640
TOKENS = LAT_CELLS * LON_CELLS
N_LON, N_LAT = 32, 4
PAIRS = HEAD_COUNT // 2
POLAR = (0, 3)
INNER = (1, 2)
AXES = ("lon", "lat")
norm_epsilon = 1e-05
attention_scale = 0.125
F32, BF16 = jnp.float32, jnp.bfloat16
VMEM_LIMIT = 32 * 1024 * 1024


def time_vector(timestep, time_weight):
    half_width = TIME_WIDTH // 2
    frequency = jnp.exp(-math.log(10000.0) * jnp.arange(half_width, dtype=F32) / half_width)
    angles = timestep.astype(F32)[0] * frequency
    embedding = jnp.concatenate([jnp.cos(angles), jnp.sin(angles)])
    return jnp.dot(
        embedding[None, :], time_weight, precision=lax.Precision.HIGHEST, preferred_element_type=F32
    )


def send(value, target, bands=range(N_LAT)):
    pairs = [
        (p * N_LAT + b, (target(p, b) if b in bands else p) * N_LAT + b)
        for p in range(N_LON)
        for b in range(N_LAT)
    ]
    return lax.ppermute(value, AXES, pairs)


def send_band(value, moves):
    pairs = [(p * N_LAT + b, p * N_LAT + c) for p in range(N_LON) for b, c in moves]
    return lax.ppermute(value, AXES, pairs)


def partner(p, band=0):
    return p ^ 1


def aside(p, band=0):
    return (p + (-1 if p % 2 == 0 else 1)) % N_LON


def ahead(p, band=0):
    return (p + (2 if p % 2 == 0 else -2)) % N_LON


def behind(p, band=0):
    return (p + (-2 if p % 2 == 0 else 2)) % N_LON


def ring_x(steps):
    return lambda p, band: (p - 8 * steps) % N_LON


def ring_z(steps):
    return lambda p, band: p // 8 * 8 + (p % 8 - 2 * steps) % 8


def whole(*shape):
    return pl.BlockSpec(shape, lambda i: (0,) * len(shape))


N_MASKS = 28
X_MASKS, Z_MASKS, Y_MASKS, NEAR, FAR = 0, 8, 16, 20, 24


def prepare_kernel(place, links_ref, left_ref, right_ref, top_ref, low_ref, mask_ref, wide_ref):
    lon, band = place[0], place[1]
    parity, here_z = lon % 2, lon // 2 % 4

    def put(at, value):
        mask_ref[at : at + 1] = jnp.broadcast_to(value.astype(F32), (1, CHANNELS))

    for way in range(2):
        target = jnp.minimum(band + 1, N_LAT - 1) if way == 0 else jnp.maximum(band - 1, 0)
        links = links_ref[target]
        link = jnp.broadcast_to(links[0:1, way : way + 1], (1, CHANNELS))
        shift = jnp.where(link < 0, link + N_LON, link)
        shift_x, shift_z, shift_y = shift >> 3, (shift >> 1) & 3, shift & 1
        carry_y = (((parity + shift_y) & 1) + shift_y) >> 1
        final_z = (here_z + 8 - shift_z - carry_y) & 3
        carry_z = (final_z + shift_z + carry_y) >> 2
        move_x = (shift_x + carry_z) & 3
        move_z = (shift_z + carry_y) & 3
        for step in range(4):
            put(X_MASKS + 2 * step + way, move_x == step)
            put(Z_MASKS + 2 * step + way, move_z == step)
        own = jnp.broadcast_to(links_ref[band][0:1, way : way + 1], (1, CHANNELS))
        for step in range(2):
            put(Y_MASKS + 2 * step + way, (own & 1) == step)
    flat = lambda value: jnp.full((1, CHANNELS), value.astype(F32), F32)
    put(NEAR, flat(band % 2 == 0))
    put(NEAR + 1, flat(band % 2 == 1))
    put(NEAR + 2, flat(band % 2 == 1))
    put(NEAR + 3, flat(band % 2 == 0))
    put(FAR, flat(band == 1))
    put(FAR + 1, flat(band == 2))
    put(FAR + 2, flat(band == 2))
    put(FAR + 3, flat(band == 1))
    for way, (row_ref, at) in enumerate(((low_ref, LAT_CELLS - 1), (top_ref, 0))):
        wide_ref[way, 0:LON_CELLS] = row_ref[0]
        corners = [ref[at].astype(F32) for ref in (left_ref, right_ref)]
        wide_ref[way, LON_CELLS : LON_CELLS + 2] = jnp.concatenate(corners, 0).astype(BF16)


def prepare(place, neighbors, left, right, stale):
    row = lambda at: pl.BlockSpec((1, LON_CELLS, CHANNELS), lambda i: (at, 0, 0))
    return pl.pallas_call(
        prepare_kernel,
        grid=(1,),
        in_specs=[
            pl.BlockSpec(memory_space=pltpu.SMEM),
            whole(N_LAT, N_LON, 2),
            whole(LAT_CELLS, 1, CHANNELS),
            whole(LAT_CELLS, 1, CHANNELS),
            row(0),
            row(LAT_CELLS - 1),
        ],
        out_specs=[whole(N_MASKS, CHANNELS), whole(2, LON_CELLS + 2, CHANNELS)],
        out_shape=[
            jax.ShapeDtypeStruct((N_MASKS, CHANNELS), F32),
            jax.ShapeDtypeStruct((2, LON_CELLS + 2, CHANNELS), BF16),
        ],
        name="prepare",
    )(place, neighbors, left, right, stale, stale)


def flags_kernel(place, readers_ref, flag_ref):
    lon, band = place[0], place[1]
    side = 1 - 2 * (lon % 2)
    polar = (band == 0) | (band == N_LAT - 1)
    hit = (readers_ref[band] == lon).astype(jnp.int32)
    row = lax.broadcasted_iota(jnp.int32, hit.shape, 0)

    def reads(steps):
        source = (lon + side * steps + N_LON) % N_LON
        return jnp.max(jnp.where(row == source, hit, 0))

    only_polar = polar.astype(jnp.int32)
    flag_ref[0] = 1
    flag_ref[1] = reads(1)
    flag_ref[2] = reads(-2)
    flag_ref[3] = reads(2)
    flag_ref[4] = reads(-1) * only_polar
    flag_ref[5] = reads(3) * only_polar
    flag_ref[6] = jnp.where(polar, reads(-3), reads(-1))
    flag_ref[7] = only_polar


def flags_of(place, readers):
    smem = pl.BlockSpec(memory_space=pltpu.SMEM)
    return pl.pallas_call(
        flags_kernel,
        in_specs=[smem, pl.BlockSpec(memory_space=pltpu.VMEM)],
        out_specs=smem,
        out_shape=jax.ShapeDtypeStruct((8,), jnp.int32),
        name="flags",
    )(place, readers)


def conv_kernel(left_ref, right_ref, latent_ref, w_any, out_ref, x_s, w_s, sems):
    copies = [pltpu.make_async_copy(w_any.at[i], w_s.at[i], sems.at[i]) for i in range(3)]
    for i in (1, 0, 2):
        copies[i].start()
    column = lax.broadcasted_iota(jnp.int32, (LON_CELLS, CHANNELS), 0)
    for r in range(LAT_CELLS):
        rows = slice(r * LON_CELLS, (r + 1) * LON_CELLS)
        cells = latent_ref[r]
        x_s[rows, CHANNELS : 2 * CHANNELS] = cells
        wide = cells.astype(F32)
        before = jnp.where(column == 0, left_ref[r].astype(F32), pltpu.roll(wide, 1, 0))
        after = jnp.where(
            column == LON_CELLS - 1, right_ref[r].astype(F32), pltpu.roll(wide, LON_CELLS - 1, 0)
        )
        x_s[rows, :CHANNELS] = before.astype(BF16)
        x_s[rows, 2 * CHANNELS :] = after.astype(BF16)
    copies[1].wait()
    for m in range(0, TOKENS, 256):
        out_ref[m : m + 256] = jnp.dot(x_s[m : m + 256], w_s[1], preferred_element_type=F32)
    copies[0].wait()
    for m in (0, 240):
        out_ref[m + 32 : m + 272] += jnp.dot(x_s[m : m + 240], w_s[0], preferred_element_type=F32)
    copies[2].wait()
    for m in (0, 240):
        out_ref[m : m + 240] += jnp.dot(x_s[m + 32 : m + 272], w_s[2], preferred_element_type=F32)


def conv(left, right, latent, w):
    return pl.pallas_call(
        conv_kernel,
        grid=(1,),
        in_specs=[
            whole(LAT_CELLS, 1, CHANNELS),
            whole(LAT_CELLS, 1, CHANNELS),
            whole(LAT_CELLS, LON_CELLS, CHANNELS),
            pl.BlockSpec(memory_space=pl.ANY),
        ],
        out_specs=whole(TOKENS, CHANNELS),
        out_shape=jax.ShapeDtypeStruct((TOKENS, CHANNELS), F32),
        scratch_shapes=[
            pltpu.VMEM((TOKENS, 3 * CHANNELS), BF16),
            pltpu.VMEM((3, 3 * CHANNELS, CHANNELS), BF16),
            pltpu.SemaphoreType.DMA((3,)),
        ],
        compiler_params=pltpu.CompilerParams(vmem_limit_bytes=54 * 1024 * 1024),
        cost_estimate=cost(1),
        name="conv",
    )(left, right, latent, w)


def dense_kernel(
    rim_ref,
    lift_ref,
    gain_ref,
    w_any,
    acc_any,
    latent_any,
    qkv_any,
    mixed_any,
    q_any,
    kv_any,
    acc_ref,
    latent_ref,
    qkv_ref,
    w_ref,
    mixed_ref,
    q_ref,
    kv_ref,
    sems,
    out_sems,
):
    half = TOKENS // 4
    middle, top, low = pl.ds(half, 2 * half), pl.ds(0, half), pl.ds(3 * half, half)
    lane_low = lax.broadcasted_iota(jnp.int32, (half, 128), 1) < HEAD_SIZE
    copies = []

    def fetch(source, target):
        copies.append(pltpu.make_async_copy(source, target, sems.at[len(copies)]))
        copies[-1].start()

    for some in (middle, None, top, low):
        if some is None:
            fetch(qkv_any, qkv_ref)
            fetch(w_any.at[0], w_ref.at[0])
            fetch(w_any.at[2], w_ref.at[1])
        else:
            fetch(acc_any.at[some], acc_ref.at[some])
            fetch(latent_any.at[some], latent_ref.at[some])
    acc_mid, latent_mid, qkv_in, w_top, w_low, acc_top, latent_top, acc_low, latent_low = copies

    def norm(m, lifted):
        rows = slice(m, m + half)
        mixed = (latent_ref[rows].astype(F32) + jax.nn.silu(lifted + lift_ref[...])).astype(BF16)
        mixed_ref[rows] = mixed
        flat = mixed.astype(F32)
        mean = jnp.mean(flat, axis=-1, keepdims=True)
        centered = flat - mean
        var = jnp.mean(centered * centered, axis=-1, keepdims=True)
        return (centered * lax.rsqrt(var + norm_epsilon) * gain_ref[...]).astype(BF16)

    leaving = []

    def project(normed, starts):
        both = jnp.dot(jnp.concatenate(normed, 0), qkv_ref[...], preferred_element_type=F32)
        for i, m in enumerate(starts):
            rows = slice(m, m + half)
            out = both[i * half : (i + 1) * half]
            q = out[:, :CHANNELS].astype(BF16).astype(F32) * attention_scale
            for j in range(PAIRS):
                two = q[:, 128 * j : 128 * j + 128]
                q_ref[2 * j, rows] = jnp.where(lane_low, two, 0.0).astype(BF16)
                q_ref[2 * j + 1, rows] = jnp.where(lane_low, 0.0, two).astype(BF16)
            for at in range(2):
                kv_ref[at, rows] = out[:, (at + 1) * CHANNELS : (at + 2) * CHANNELS].astype(BF16)
            some = pl.ds(m, half)
            for source, target in (
                (mixed_ref.at[some], mixed_any.at[some]),
                (q_ref.at[:, some], q_any.at[:, some]),
                (kv_ref.at[:, some], kv_any.at[:, some]),
            ):
                leaving.append(pltpu.make_async_copy(source, target, out_sems.at[len(leaving)]))
                leaving[-1].start()

    acc_mid.wait()
    latent_mid.wait()
    normed = [norm(m, acc_ref[m : m + half]) for m in (half, 2 * half)]
    qkv_in.wait()
    project(normed, (half, 2 * half))
    w_top.wait()
    edge_top = jnp.dot(rim_ref[:LON_CELLS], w_ref[0], preferred_element_type=F32)
    w_low.wait()
    edge_low = jnp.dot(rim_ref[LON_CELLS:], w_ref[1], preferred_element_type=F32)
    for copy in (acc_top, latent_top, acc_low, latent_low):
        copy.wait()
    rows = acc_ref[:half]
    normed = [norm(0, jnp.concatenate([rows[:LON_CELLS] + edge_top, rows[LON_CELLS:]], 0))]
    rows = acc_ref[3 * half :]
    normed.append(norm(3 * half, jnp.concatenate([rows[:-LON_CELLS], rows[-LON_CELLS:] + edge_low], 0)))
    project(normed, (0, 3 * half))
    for copy in leaving:
        copy.wait()


def dense(rims, w, acc, lift, latent, gain, qkv):
    vmem, anywhere = pl.BlockSpec(memory_space=pltpu.VMEM), pl.BlockSpec(memory_space=pl.ANY)
    outs = [(TOKENS, CHANNELS), (HEAD_COUNT, TOKENS, 128), (2, TOKENS, CHANNELS)]
    return pl.pallas_call(
        dense_kernel,
        in_specs=[vmem] * 3 + [anywhere] * 4,
        out_specs=[anywhere] * 3,
        out_shape=[jax.ShapeDtypeStruct(shape, BF16) for shape in outs],
        scratch_shapes=[
            pltpu.VMEM((TOKENS, CHANNELS), F32),
            pltpu.VMEM((TOKENS, CHANNELS), BF16),
            pltpu.VMEM((CHANNELS, 3 * CHANNELS), BF16),
            pltpu.VMEM((2, 3 * CHANNELS, CHANNELS), BF16),
        ]
        + [pltpu.VMEM(shape, BF16) for shape in outs]
        + [pltpu.SemaphoreType.DMA((9,)), pltpu.SemaphoreType.DMA((12,))],
        compiler_params=pltpu.CompilerParams(vmem_limit_bytes=54 * 1024 * 1024),
        cost_estimate=cost(0.01),
        name="dense",
    )(rims, lift, gain, w, acc, latent, qkv)


LEAST, MOST = 1e-18, 1e18


def add_tile(flag, q_ref, k_ref, v_ref, acc_ref, fresh):
    k, v = k_ref[0], v_ref[0]
    one = jnp.ones((TOKENS, 128), BF16)
    if flag is not None:
        read = flag != 0
        k = jnp.where(read, k, jnp.zeros_like(k))
        v = jnp.where(read, v, jnp.zeros_like(v))
        one = jnp.where(read, one, jnp.zeros_like(one))
    k_t = k.T
    v_one = jnp.concatenate([v, one], 1)
    low = lax.broadcasted_iota(jnp.int32, (TOKENS, 128), 1) < HEAD_SIZE
    parts = []
    for head in range(2):
        scores = jnp.dot(q_ref[head], k_t, preferred_element_type=F32)
        parts.append(jnp.dot(jnp.exp(scores).astype(BF16), v_one, preferred_element_type=F32))
    part = jnp.concatenate(
        [
            jnp.where(low, parts[0][:, :128], parts[1][:, :128]),
            jnp.where(low, parts[0][:, 128:], parts[1][:, 128:]),
        ],
        1,
    )
    if fresh:
        acc_ref[0] = part
    else:
        acc_ref[0] += part


def attend_kernel(count, offset, first, *refs):
    refs = list(refs)
    flags, q_ref = refs.pop(0), refs.pop(0)
    tiles = [(refs.pop(0), refs.pop(0)) for _ in range(count)]
    acc_ref = refs[-1]
    if not first:
        acc_ref[...] = refs[0][...]
    for t, (k_ref, v_ref) in enumerate(tiles):
        own = first and t == 0
        add_tile(None if own else flags[offset + t], q_ref, k_ref, v_ref, acc_ref, own)


def redo_pair(j, flags, q_any, tiles, q_s, k_s, v_s, m_s, a_s, att_ref, sem):
    columns = pl.ds(pl.multiple_of(j * 128, 128), 128)
    block = 128
    low = lax.broadcasted_iota(jnp.int32, (block, 128), 1) < HEAD_SIZE

    def fetch(source, target):
        copy = pltpu.make_async_copy(source, target, sem)
        copy.start()
        copy.wait()

    fetch(q_any.at[pl.ds(2 * j, 2)], q_s)
    m_s[...] = jnp.full((TOKENS, 128), -1e30, F32)
    a_s[...] = jnp.zeros((TOKENS, 256), F32)
    for t, tile in enumerate(tiles):

        @pl.when(flags[t] != 0)
        def _(tile=tile):
            k_any, k_at, v_any, v_at = tile
            fetch(k_any.at[k_at, :, columns], k_s)
            fetch(v_any.at[v_at, :, columns], v_s)

            def rows_step(i, carry):
                rows = pl.ds(pl.multiple_of(i * block, block), block)
                v_one = jnp.concatenate([v_s[...], jnp.ones((TOKENS, 128), BF16)], 1)
                nt = (((1,), (1,)), ((), ()))
                old = m_s[rows]
                tops, parts = [], []
                for head in range(2):
                    scores = lax.dot_general(q_s[head, rows], k_s[...], nt, preferred_element_type=F32)
                    top = jnp.maximum(
                        jnp.max(scores, axis=-1, keepdims=True), old[:, 64 * head : 64 * head + 1]
                    )
                    p = jnp.exp(scores - top).astype(BF16)
                    tops.append(top)
                    parts.append(jnp.dot(p, v_one, preferred_element_type=F32))
                new = jnp.where(low, tops[0], tops[1])
                fade = jnp.exp(old - new)
                part = jnp.concatenate(
                    [
                        jnp.where(low, parts[0][:, :128], parts[1][:, :128]),
                        jnp.where(low, parts[0][:, 128:], parts[1][:, 128:]),
                    ],
                    1,
                )
                a_s[rows] = a_s[rows] * jnp.concatenate([fade, fade], 1) + part
                m_s[rows] = new
                return carry

            lax.fori_loop(0, TOKENS // block, rows_step, 0)

    att_ref[:, columns] = (a_s[:, :128] / a_s[:, 128:]).astype(BF16)


def finish_kernel(count, offset, places, *refs):
    refs = list(refs)
    flags, q_ref = refs.pop(0), refs.pop(0)
    tiles = [(refs.pop(0), refs.pop(0)) for _ in range(count)]
    acc_in, mixed_ref, w_ref, q_any = refs[:4]
    every = [(refs[4 + k], k_at, refs[4 + v], v_at) for k, k_at, v, v_at in places]
    out_ref, acc_ref, att_ref, bad, q_s, k_s, v_s, m_s, a_s, sem = refs[-10:]
    j = pl.program_id(0)
    acc_ref[...] = acc_in[...]
    for t, (k_ref, v_ref) in enumerate(tiles):
        add_tile(flags[offset + t], q_ref, k_ref, v_ref, acc_ref, False)
    columns = pl.ds(pl.multiple_of(j * 128, 128), 128)
    totals = acc_ref[0, :, 128:]
    att_ref[:, columns] = (acc_ref[0, :, :128] / totals).astype(BF16)
    fine = (jnp.min(totals) > LEAST) & (jnp.max(totals) < MOST)
    bad[0] = jnp.where(j == 0, 0, bad[0]) + jnp.where(fine, 0, 1)

    @pl.when(j == PAIRS - 1)
    def _():
        @pl.when(bad[0] != 0)
        def _():
            def one_pair(i, carry):
                redo_pair(i, flags, q_any, every, q_s, k_s, v_s, m_s, a_s, att_ref, sem)
                return carry

            lax.fori_loop(0, PAIRS, one_pair, 0)

        for r in range(0, TOKENS, 256):
            rows = slice(r, r + 256)
            add = jnp.dot(att_ref[rows], w_ref[...], preferred_element_type=F32)
            out_ref[rows] = (mixed_ref[rows].astype(F32) + add).astype(BF16)


ACC_SPEC = pl.BlockSpec((1, TOKENS, 256), lambda j: (j, 0, 0))
ACC_SHAPE = jax.ShapeDtypeStruct((PAIRS, TOKENS, 256), F32)


def tile_specs(flags, q, tiles):
    specs = [
        pl.BlockSpec(memory_space=pltpu.SMEM),
        pl.BlockSpec((2, TOKENS, 128), lambda j: (j, 0, 0)),
    ]
    args = [flags, q]
    for k, k_at, v, v_at in tiles:
        specs += [
            pl.BlockSpec((1, TOKENS, 128), lambda j, at=k_at: (at, 0, j)),
            pl.BlockSpec((1, TOKENS, 128), lambda j, at=v_at: (at, 0, j)),
        ]
        args += [k, v]
    return specs, args


def one(tile):
    return tile, 0, tile, 1


def cost(n):
    return pl.CostEstimate(flops=int(n * 4_600_000_000), bytes_accessed=1_000_000, transcendentals=0)


def attend(flags, q, tiles, offset, acc=None, limit=20):
    specs, args = tile_specs(flags, q, tiles)
    if acc is not None:
        specs.append(ACC_SPEC)
        args.append(acc)
    return pl.pallas_call(
        functools.partial(attend_kernel, len(tiles), offset, acc is None),
        grid=(PAIRS,),
        in_specs=specs,
        out_specs=ACC_SPEC,
        out_shape=ACC_SHAPE,
        compiler_params=pltpu.CompilerParams(vmem_limit_bytes=limit * 1024 * 1024),
        cost_estimate=cost(0.01),
        name="attend",
    )(*args)


def finish(flags, q, tiles, offset, acc, mixed, out_weight, every):
    specs, args = tile_specs(flags, q, tiles)
    anywhere = pl.BlockSpec(memory_space=pl.ANY)
    arrays, places = [], []
    for k, k_at, v, v_at in every:
        where = []
        for array in (k, v):
            known = [i for i, other in enumerate(arrays) if other is array]
            if not known:
                arrays.append(array)
            where.append(known[0] if known else len(arrays) - 1)
        places.append((where[0], k_at, where[1], v_at))
    specs += [ACC_SPEC, whole(TOKENS, CHANNELS), whole(CHANNELS, CHANNELS)]
    specs += [anywhere] * (1 + len(arrays))
    args += [acc, mixed, out_weight, q] + arrays
    return pl.pallas_call(
        functools.partial(finish_kernel, len(tiles), offset, tuple(places)),
        grid=(PAIRS,),
        in_specs=specs,
        out_specs=whole(TOKENS, CHANNELS),
        out_shape=jax.ShapeDtypeStruct((TOKENS, CHANNELS), BF16),
        scratch_shapes=[
            pltpu.VMEM((1, TOKENS, 256), F32),
            pltpu.VMEM((TOKENS, CHANNELS), BF16),
            pltpu.SMEM((1,), jnp.int32),
            pltpu.VMEM((2, TOKENS, 128), BF16),
            pltpu.VMEM((TOKENS, 128), BF16),
            pltpu.VMEM((TOKENS, 128), BF16),
            pltpu.VMEM((TOKENS, 128), F32),
            pltpu.VMEM((TOKENS, 256), F32),
            pltpu.SemaphoreType.DMA,
        ],
        compiler_params=pltpu.CompilerParams(vmem_limit_bytes=20 * 1024 * 1024),
        cost_estimate=cost(len(tiles)),
        name="finish",
    )(*args)


def body(
    latent,
    stale,
    stale_kv,
    neighbors,
    readers,
    timestep,
    conv_weight,
    time_weight,
    norm_gain,
    qkv_weight,
    out_weight,
):
    tile = stale_kv.reshape(2, TOKENS, CHANNELS)
    weights = conv_weight.reshape(3, 3 * CHANNELS, CHANNELS)
    place = jnp.stack([lax.axis_index("lon"), lax.axis_index("lat")]).astype(jnp.int32)

    left = send(stale[:, -1:], lambda p, band: (p + 1) % N_LON)
    right = send(stale[:, :1], lambda p, band: (p - 1) % N_LON)

    tile, left, right = lax.optimization_barrier((tile, left, right))
    got_r = send(tile, partner)

    masks, wide = prepare(place, neighbors, left, right, stale)

    def choose(moved, base):
        rows = []
        for way in range(2):
            total = moved[0][way].astype(F32) * masks[base + way]
            for step in range(1, len(moved)):
                total += moved[step][way].astype(F32) * masks[base + 2 * step + way]
            rows.append(total.astype(BF16))
        return jnp.stack(rows, 0)

    def shifted(rows):
        x = jnp.concatenate([rows[:, d : d + LON_CELLS] for d in range(3)], -1)
        return x.reshape(-1, 3 * CHANNELS)

    wide = choose([wide] + [send(wide, ring_x(s)) for s in (1, 2, 3)], X_MASKS)
    wide = choose([wide] + [send(wide, ring_z(s)) for s in (1, 2, 3)], Z_MASKS)
    tile, wide, latent, readers, timestep, norm_gain = lax.optimization_barrier(
        (tile, wide, latent, readers, timestep, norm_gain)
    )
    got_f = send(tile, ahead)
    got_b = send(tile, behind)
    acc = conv(left, right, latent, weights)
    lift = time_vector(timestep, time_weight)
    flags = flags_of(place, readers)

    wide, acc, got_r, lift, flags = lax.optimization_barrier((wide, acc, got_r, lift, flags))
    both = lambda base: (wide[0].astype(F32) * masks[base] + wide[1].astype(F32) * masks[base + 1]).astype(BF16)
    near = send_band(both(NEAR), ((0, 1), (1, 0), (2, 3), (3, 2)))
    far = send_band(both(FAR), ((1, 2), (2, 1), (0, 0), (3, 3)))
    near, far = near.astype(F32), far.astype(F32)
    wide = jnp.stack(
        [(near * masks[NEAR + 2 + i] + far * masks[FAR + 2 + i]).astype(BF16) for i in range(2)], 0
    )
    swapped = send(wide, partner)
    wide = choose([wide, swapped], Y_MASKS)

    rims = shifted(
        jnp.concatenate(
            [wide[:, LON_CELLS : LON_CELLS + 1], wide[:, :LON_CELLS], wide[:, LON_CELLS + 1 :]], 1
        )
    )
    got_t = send(got_r, ahead, POLAR)
    got_u = send(got_r, behind, POLAR)
    mixed, q, fresh = dense(
        rims,
        weights,
        acc,
        lift,
        latent.reshape(TOKENS, CHANNELS),
        norm_gain[None, :],
        qkv_weight,
    )

    got_b, got_f, q = lax.optimization_barrier((got_b, got_f, q))
    got_s = send(got_b, lambda p, band: aside(p) if band in POLAR else partner(p))
    sums = attend(flags, q, [one(fresh), one(got_r)], 0)
    sums = attend(flags, q, [one(got_f), one(got_b)], 2, sums)
    sums = attend(flags, q, [one(got_t), one(got_u)], 4, sums)
    every = [one(tile) for tile in (fresh, got_r, got_f, got_b, got_t, got_u, got_s)]
    out = finish(flags, q, [one(got_s)], 6, sums, mixed, out_weight, every)
    return (
        out.reshape(LAT_CELLS, LON_CELLS, CHANNELS),
        fresh.reshape(2, LAT_CELLS, LON_CELLS, CHANNELS),
    )


def solution(mesh):
    in_specs = (
        P("lat", "lon", None),
        P("lat", "lon", None),
        P(None, "lat", "lon", None),
        P(),
        P(),
        P(),
        P(),
        P(),
        P(),
        P(),
        P(),
    )
    out_specs = (P("lat", "lon", None), P(None, "lat", "lon", None))
    return jax.shard_map(body, mesh=mesh, in_specs=in_specs, out_specs=out_specs, check_vma=False)
```

```python
import functools
import math

import jax
import jax.numpy as jnp
from jax import lax
from jax.experimental import pallas as pl
from jax.experimental.pallas import tpu as pltpu
from jax.sharding import PartitionSpec as P

HEAD_COUNT = 10
HEAD_SIZE = 64
TIME_WIDTH = 320
LAT_CELLS, LON_CELLS, CHANNELS = 16, 32, 640
TOKENS = LAT_CELLS * LON_CELLS
N_LON, N_LAT = 32, 4
PAIRS = HEAD_COUNT // 2
POLAR = (0, 3)
INNER = (1, 2)
AXES = ("lon", "lat")
norm_epsilon = 1e-05
attention_scale = 0.125
F32, BF16 = jnp.float32, jnp.bfloat16
VMEM_LIMIT = 32 * 1024 * 1024


def time_vector(timestep, time_weight):
    half_width = TIME_WIDTH // 2
    frequency = jnp.exp(-math.log(10000.0) * jnp.arange(half_width, dtype=F32) / half_width)
    angles = timestep.astype(F32)[0] * frequency
    embedding = jnp.concatenate([jnp.cos(angles), jnp.sin(angles)])
    return jnp.dot(
        embedding[None, :], time_weight, precision=lax.Precision.HIGHEST, preferred_element_type=F32
    )


def send(value, target, bands=range(N_LAT)):
    pairs = [
        (p * N_LAT + b, (target(p, b) if b in bands else p) * N_LAT + b)
        for p in range(N_LON)
        for b in range(N_LAT)
    ]
    return lax.ppermute(value, AXES, pairs)


def send_band(value, moves):
    pairs = [(p * N_LAT + b, p * N_LAT + c) for p in range(N_LON) for b, c in moves]
    return lax.ppermute(value, AXES, pairs)


def partner(p, band=0):
    return p ^ 1


def aside(p, band=0):
    return (p + (-1 if p % 2 == 0 else 1)) % N_LON


def ahead(p, band=0):
    return (p + (2 if p % 2 == 0 else -2)) % N_LON


def behind(p, band=0):
    return (p + (-2 if p % 2 == 0 else 2)) % N_LON


def ring_x(steps):
    return lambda p, band: (p - 8 * steps) % N_LON


def ring_z(steps):
    return lambda p, band: p // 8 * 8 + (p % 8 - 2 * steps) % 8


def whole(*shape):
    return pl.BlockSpec(shape, lambda i: (0,) * len(shape))


N_MASKS = 28
X_MASKS, Z_MASKS, Y_MASKS, NEAR, FAR = 0, 8, 16, 20, 24


def prepare_kernel(place, links_ref, left_ref, right_ref, top_ref, low_ref, mask_ref, wide_ref):
    lon, band = place[0], place[1]
    parity, here_z = lon % 2, lon // 2 % 4

    def put(at, value):
        mask_ref[at : at + 1] = jnp.broadcast_to(value.astype(F32), (1, CHANNELS))

    for way in range(2):
        target = jnp.minimum(band + 1, N_LAT - 1) if way == 0 else jnp.maximum(band - 1, 0)
        links = links_ref[target]
        link = jnp.broadcast_to(links[0:1, way : way + 1], (1, CHANNELS))
        shift = jnp.where(link < 0, link + N_LON, link)
        shift_x, shift_z, shift_y = shift >> 3, (shift >> 1) & 3, shift & 1
        carry_y = (((parity + shift_y) & 1) + shift_y) >> 1
        final_z = (here_z + 8 - shift_z - carry_y) & 3
        carry_z = (final_z + shift_z + carry_y) >> 2
        move_x = (shift_x + carry_z) & 3
        move_z = (shift_z + carry_y) & 3
        for step in range(4):
            put(X_MASKS + 2 * step + way, move_x == step)
            put(Z_MASKS + 2 * step + way, move_z == step)
        own = jnp.broadcast_to(links_ref[band][0:1, way : way + 1], (1, CHANNELS))
        for step in range(2):
            put(Y_MASKS + 2 * step + way, (own & 1) == step)
    flat = lambda value: jnp.full((1, CHANNELS), value.astype(F32), F32)
    put(NEAR, flat(band % 2 == 0))
    put(NEAR + 1, flat(band % 2 == 1))
    put(NEAR + 2, flat(band % 2 == 1))
    put(NEAR + 3, flat(band % 2 == 0))
    put(FAR, flat(band == 1))
    put(FAR + 1, flat(band == 2))
    put(FAR + 2, flat(band == 2))
    put(FAR + 3, flat(band == 1))
    for way, (row_ref, at) in enumerate(((low_ref, LAT_CELLS - 1), (top_ref, 0))):
        wide_ref[way, 0:LON_CELLS] = row_ref[0]
        corners = [ref[at].astype(F32) for ref in (left_ref, right_ref)]
        wide_ref[way, LON_CELLS : LON_CELLS + 2] = jnp.concatenate(corners, 0).astype(BF16)


def prepare(place, neighbors, left, right, stale):
    row = lambda at: pl.BlockSpec((1, LON_CELLS, CHANNELS), lambda i: (at, 0, 0))
    return pl.pallas_call(
        prepare_kernel,
        grid=(1,),
        in_specs=[
            pl.BlockSpec(memory_space=pltpu.SMEM),
            whole(N_LAT, N_LON, 2),
            whole(LAT_CELLS, 1, CHANNELS),
            whole(LAT_CELLS, 1, CHANNELS),
            row(0),
            row(LAT_CELLS - 1),
        ],
        out_specs=[whole(N_MASKS, CHANNELS), whole(2, LON_CELLS + 2, CHANNELS)],
        out_shape=[
            jax.ShapeDtypeStruct((N_MASKS, CHANNELS), F32),
            jax.ShapeDtypeStruct((2, LON_CELLS + 2, CHANNELS), BF16),
        ],
        name="prepare",
    )(place, neighbors, left, right, stale, stale)


def flags_kernel(place, readers_ref, flag_ref):
    lon, band = place[0], place[1]
    side = 1 - 2 * (lon % 2)
    polar = (band == 0) | (band == N_LAT - 1)
    hit = (readers_ref[band] == lon).astype(jnp.int32)
    row = lax.broadcasted_iota(jnp.int32, hit.shape, 0)

    def reads(steps):
        source = (lon + side * steps + N_LON) % N_LON
        return jnp.max(jnp.where(row == source, hit, 0))

    only_polar = polar.astype(jnp.int32)
    flag_ref[0] = 1
    flag_ref[1] = reads(1)
    flag_ref[2] = reads(-2)
    flag_ref[3] = reads(2)
    flag_ref[4] = reads(-1) * only_polar
    flag_ref[5] = reads(3) * only_polar
    flag_ref[6] = jnp.where(polar, reads(-3), reads(-1))
    flag_ref[7] = only_polar


def flags_of(place, readers):
    smem = pl.BlockSpec(memory_space=pltpu.SMEM)
    return pl.pallas_call(
        flags_kernel,
        in_specs=[smem, pl.BlockSpec(memory_space=pltpu.VMEM)],
        out_specs=smem,
        out_shape=jax.ShapeDtypeStruct((8,), jnp.int32),
        name="flags",
    )(place, readers)


def conv_kernel(left_ref, right_ref, latent_ref, w_any, out_ref, x_s, w_s, sems):
    copies = [pltpu.make_async_copy(w_any.at[i], w_s.at[i], sems.at[i]) for i in range(3)]
    for i in (1, 0, 2):
        copies[i].start()
    column = lax.broadcasted_iota(jnp.int32, (LON_CELLS, CHANNELS), 0)
    for r in range(LAT_CELLS):
        rows = slice(r * LON_CELLS, (r + 1) * LON_CELLS)
        cells = latent_ref[r]
        x_s[rows, CHANNELS : 2 * CHANNELS] = cells
        wide = cells.astype(F32)
        before = jnp.where(column == 0, left_ref[r].astype(F32), pltpu.roll(wide, 1, 0))
        after = jnp.where(
            column == LON_CELLS - 1, right_ref[r].astype(F32), pltpu.roll(wide, LON_CELLS - 1, 0)
        )
        x_s[rows, :CHANNELS] = before.astype(BF16)
        x_s[rows, 2 * CHANNELS :] = after.astype(BF16)
    copies[1].wait()
    for m in range(0, TOKENS, 256):
        out_ref[m : m + 256] = jnp.dot(x_s[m : m + 256], w_s[1], preferred_element_type=F32)
    copies[0].wait()
    for m in (0, 240):
        out_ref[m + 32 : m + 272] += jnp.dot(x_s[m : m + 240], w_s[0], preferred_element_type=F32)
    copies[2].wait()
    for m in (0, 240):
        out_ref[m : m + 240] += jnp.dot(x_s[m + 32 : m + 272], w_s[2], preferred_element_type=F32)


def conv(left, right, latent, w):
    return pl.pallas_call(
        conv_kernel,
        grid=(1,),
        in_specs=[
            whole(LAT_CELLS, 1, CHANNELS),
            whole(LAT_CELLS, 1, CHANNELS),
            whole(LAT_CELLS, LON_CELLS, CHANNELS),
            pl.BlockSpec(memory_space=pl.ANY),
        ],
        out_specs=whole(TOKENS, CHANNELS),
        out_shape=jax.ShapeDtypeStruct((TOKENS, CHANNELS), F32),
        scratch_shapes=[
            pltpu.VMEM((TOKENS, 3 * CHANNELS), BF16),
            pltpu.VMEM((3, 3 * CHANNELS, CHANNELS), BF16),
            pltpu.SemaphoreType.DMA((3,)),
        ],
        compiler_params=pltpu.CompilerParams(vmem_limit_bytes=54 * 1024 * 1024),
        cost_estimate=cost(1),
        name="conv",
    )(left, right, latent, w)


def dense_kernel(
    rim_ref,
    lift_ref,
    w_any,
    acc_any,
    latent_any,
    qkv_any,
    mixed_any,
    q_any,
    kv_any,
    acc_ref,
    latent_ref,
    qkv_ref,
    w_ref,
    mixed_ref,
    q_ref,
    kv_ref,
    sems,
    out_sems,
):
    half = TOKENS // 4
    middle, top, low = pl.ds(half, 2 * half), pl.ds(0, half), pl.ds(3 * half, half)
    lane_low = lax.broadcasted_iota(jnp.int32, (half, 128), 1) < HEAD_SIZE
    copies = []

    def fetch(source, target):
        copies.append(pltpu.make_async_copy(source, target, sems.at[len(copies)]))
        copies[-1].start()

    for some in (middle, None, top, low):
        if some is None:
            fetch(qkv_any, qkv_ref)
            fetch(w_any.at[0], w_ref.at[0])
            fetch(w_any.at[2], w_ref.at[1])
        else:
            fetch(acc_any.at[some], acc_ref.at[some])
            fetch(latent_any.at[some], latent_ref.at[some])
    acc_mid, latent_mid, qkv_in, w_top, w_low, acc_top, latent_top, acc_low, latent_low = copies

    def norm(m, lifted):
        rows = slice(m, m + half)
        mixed = (latent_ref[rows].astype(F32) + jax.nn.silu(lifted + lift_ref[0:1])).astype(BF16)
        mixed_ref[rows] = mixed
        flat = mixed.astype(F32)
        mean = jnp.mean(flat, axis=-1, keepdims=True)
        centered = flat - mean
        var = jnp.mean(centered * centered, axis=-1, keepdims=True)
        return (centered * lax.rsqrt(var + norm_epsilon) * lift_ref[1:2]).astype(BF16)

    leaving = []

    def project(normed, starts):
        both = jnp.dot(jnp.concatenate(normed, 0), qkv_ref[...], preferred_element_type=F32)
        for i, m in enumerate(starts):
            rows = slice(m, m + half)
            out = both[i * half : (i + 1) * half]
            q = out[:, :CHANNELS].astype(BF16).astype(F32) * attention_scale
            for j in range(PAIRS):
                two = q[:, 128 * j : 128 * j + 128]
                q_ref[2 * j, rows] = jnp.where(lane_low, two, 0.0).astype(BF16)
                q_ref[2 * j + 1, rows] = jnp.where(lane_low, 0.0, two).astype(BF16)
            for at in range(2):
                kv_ref[at, rows] = out[:, (at + 1) * CHANNELS : (at + 2) * CHANNELS].astype(BF16)
            some = pl.ds(m, half)
            for source, target in (
                (mixed_ref.at[some], mixed_any.at[some]),
                (q_ref.at[:, some], q_any.at[:, some]),
                (kv_ref.at[:, some], kv_any.at[:, some]),
            ):
                leaving.append(pltpu.make_async_copy(source, target, out_sems.at[len(leaving)]))
                leaving[-1].start()

    acc_mid.wait()
    latent_mid.wait()
    normed = [norm(m, acc_ref[m : m + half]) for m in (half, 2 * half)]
    qkv_in.wait()
    project(normed, (half, 2 * half))
    w_top.wait()
    edge_top = jnp.dot(rim_ref[:LON_CELLS], w_ref[0], preferred_element_type=F32)
    w_low.wait()
    edge_low = jnp.dot(rim_ref[LON_CELLS:], w_ref[1], preferred_element_type=F32)
    for copy in (acc_top, latent_top, acc_low, latent_low):
        copy.wait()
    rows = acc_ref[:half]
    normed = [norm(0, jnp.concatenate([rows[:LON_CELLS] + edge_top, rows[LON_CELLS:]], 0))]
    rows = acc_ref[3 * half :]
    normed.append(norm(3 * half, jnp.concatenate([rows[:-LON_CELLS], rows[-LON_CELLS:] + edge_low], 0)))
    project(normed, (0, 3 * half))
    for copy in leaving:
        copy.wait()


def dense(rims, w, acc, lift, latent, qkv):
    vmem, anywhere = pl.BlockSpec(memory_space=pltpu.VMEM), pl.BlockSpec(memory_space=pl.ANY)
    outs = [(TOKENS, CHANNELS), (HEAD_COUNT, TOKENS, 128), (2, TOKENS, CHANNELS)]
    return pl.pallas_call(
        dense_kernel,
        in_specs=[vmem] * 2 + [anywhere] * 4,
        out_specs=[anywhere] * 3,
        out_shape=[jax.ShapeDtypeStruct(shape, BF16) for shape in outs],
        scratch_shapes=[
            pltpu.VMEM((TOKENS, CHANNELS), F32),
            pltpu.VMEM((TOKENS, CHANNELS), BF16),
            pltpu.VMEM((CHANNELS, 3 * CHANNELS), BF16),
            pltpu.VMEM((2, 3 * CHANNELS, CHANNELS), BF16),
        ]
        + [pltpu.VMEM(shape, BF16) for shape in outs]
        + [pltpu.SemaphoreType.DMA((9,)), pltpu.SemaphoreType.DMA((12,))],
        compiler_params=pltpu.CompilerParams(vmem_limit_bytes=54 * 1024 * 1024),
        cost_estimate=cost(0.01),
        name="dense",
    )(rims, lift, w, acc, latent, qkv)


LEAST, MOST = 1e-18, 1e18


def add_tile(flag, q_ref, k_ref, v_ref, acc_ref, fresh, base_ref=None):
    k, v = k_ref[0], v_ref[0]
    one = jnp.ones((TOKENS, 128), BF16)
    if flag is not None:
        read = flag != 0
        k = jnp.where(read, k, jnp.zeros_like(k))
        v = jnp.where(read, v, jnp.zeros_like(v))
        one = jnp.where(read, one, jnp.zeros_like(one))
    k_t = k.T
    v_one = jnp.concatenate([v, one], 1)
    low = lax.broadcasted_iota(jnp.int32, (TOKENS, 128), 1) < HEAD_SIZE
    parts = []
    for head in range(2):
        scores = jnp.dot(q_ref[head], k_t, preferred_element_type=F32)
        parts.append(jnp.dot(jnp.exp(scores).astype(BF16), v_one, preferred_element_type=F32))
    part = jnp.concatenate(
        [
            jnp.where(low, parts[0][:, :128], parts[1][:, :128]),
            jnp.where(low, parts[0][:, 128:], parts[1][:, 128:]),
        ],
        1,
    )
    if fresh:
        acc_ref[0] = part
    else:
        acc_ref[0] = (acc_ref if base_ref is None else base_ref)[0] + part


def attend_kernel(count, offset, first, *refs):
    refs = list(refs)
    flags, q_ref = refs.pop(0), refs.pop(0)
    tiles = [(refs.pop(0), refs.pop(0)) for _ in range(count)]
    acc_ref = refs[-1]
    for t, (k_ref, v_ref) in enumerate(tiles):
        own = first and t == 0
        base_ref = refs[0] if t == 0 and not first else None
        add_tile(None if own else flags[offset + t], q_ref, k_ref, v_ref, acc_ref, own, base_ref)


def redo_pair(j, flags, q_any, tiles, q_s, k_s, v_s, m_s, a_s, att_ref, sem):
    columns = pl.ds(pl.multiple_of(j * 128, 128), 128)
    block = 128
    low = lax.broadcasted_iota(jnp.int32, (block, 128), 1) < HEAD_SIZE

    def fetch(source, target):
        copy = pltpu.make_async_copy(source, target, sem)
        copy.start()
        copy.wait()

    fetch(q_any.at[pl.ds(2 * j, 2)], q_s)
    m_s[...] = jnp.full((TOKENS, 128), -1e30, F32)
    a_s[...] = jnp.zeros((TOKENS, 256), F32)
    for t, tile in enumerate(tiles):

        @pl.when(flags[t] != 0)
        def _(tile=tile):
            k_any, k_at, v_any, v_at = tile
            fetch(k_any.at[k_at, :, columns], k_s)
            fetch(v_any.at[v_at, :, columns], v_s)

            def rows_step(i, carry):
                rows = pl.ds(pl.multiple_of(i * block, block), block)
                v_one = jnp.concatenate([v_s[...], jnp.ones((TOKENS, 128), BF16)], 1)
                nt = (((1,), (1,)), ((), ()))
                old = m_s[rows]
                tops, parts = [], []
                for head in range(2):
                    scores = lax.dot_general(q_s[head, rows], k_s[...], nt, preferred_element_type=F32)
                    top = jnp.maximum(
                        jnp.max(scores, axis=-1, keepdims=True), old[:, 64 * head : 64 * head + 1]
                    )
                    p = jnp.exp(scores - top).astype(BF16)
                    tops.append(top)
                    parts.append(jnp.dot(p, v_one, preferred_element_type=F32))
                new = jnp.where(low, tops[0], tops[1])
                fade = jnp.exp(old - new)
                part = jnp.concatenate(
                    [
                        jnp.where(low, parts[0][:, :128], parts[1][:, :128]),
                        jnp.where(low, parts[0][:, 128:], parts[1][:, 128:]),
                    ],
                    1,
                )
                a_s[rows] = a_s[rows] * jnp.concatenate([fade, fade], 1) + part
                m_s[rows] = new
                return carry

            lax.fori_loop(0, TOKENS // block, rows_step, 0)

    att_ref[:, columns] = (a_s[:, :128] / a_s[:, 128:]).astype(BF16)


def finish_kernel(count, offset, places, *refs):
    refs = list(refs)
    flags, q_ref = refs.pop(0), refs.pop(0)
    tiles = [(refs.pop(0), refs.pop(0)) for _ in range(count)]
    acc_in, mixed_ref, w_ref, q_any = refs[:4]
    every = [(refs[4 + k], k_at, refs[4 + v], v_at) for k, k_at, v, v_at in places]
    out_ref, acc_ref, att_ref, bad, q_s, k_s, v_s, m_s, a_s, sem = refs[-10:]
    j = pl.program_id(0)
    for t, (k_ref, v_ref) in enumerate(tiles):
        add_tile(flags[offset + t], q_ref, k_ref, v_ref, acc_ref, False, acc_in if t == 0 else None)
    columns = pl.ds(pl.multiple_of(j * 128, 128), 128)
    totals = acc_ref[0, :, 128:]
    att_ref[:, columns] = (acc_ref[0, :, :128] / totals).astype(BF16)
    fine = (jnp.min(totals) > LEAST) & (jnp.max(totals) < MOST)
    bad[0] = jnp.where(j == 0, 0, bad[0]) + jnp.where(fine, 0, 1)

    @pl.when(j == PAIRS - 1)
    def _():
        @pl.when(bad[0] != 0)
        def _():
            def one_pair(i, carry):
                redo_pair(i, flags, q_any, every, q_s, k_s, v_s, m_s, a_s, att_ref, sem)
                return carry

            lax.fori_loop(0, PAIRS, one_pair, 0)

        for r in range(0, TOKENS, 256):
            rows = slice(r, r + 256)
            add = jnp.dot(att_ref[rows], w_ref[...], preferred_element_type=F32)
            out_ref[rows] = (mixed_ref[rows].astype(F32) + add).astype(BF16)


ACC_SPEC = pl.BlockSpec((1, TOKENS, 256), lambda j: (j, 0, 0))
ACC_SHAPE = jax.ShapeDtypeStruct((PAIRS, TOKENS, 256), F32)


def tile_specs(flags, q, tiles):
    specs = [
        pl.BlockSpec(memory_space=pltpu.SMEM),
        pl.BlockSpec((2, TOKENS, 128), lambda j: (j, 0, 0)),
    ]
    args = [flags, q]
    for k, k_at, v, v_at in tiles:
        specs += [
            pl.BlockSpec((1, TOKENS, 128), lambda j, at=k_at: (at, 0, j)),
            pl.BlockSpec((1, TOKENS, 128), lambda j, at=v_at: (at, 0, j)),
        ]
        args += [k, v]
    return specs, args


def one(tile):
    return tile, 0, tile, 1


def cost(n):
    return pl.CostEstimate(flops=int(n * 4_600_000_000), bytes_accessed=1_000_000, transcendentals=0)


def attend(flags, q, tiles, offset, acc=None, limit=20):
    specs, args = tile_specs(flags, q, tiles)
    if acc is not None:
        specs.append(ACC_SPEC)
        args.append(acc)
    return pl.pallas_call(
        functools.partial(attend_kernel, len(tiles), offset, acc is None),
        grid=(PAIRS,),
        in_specs=specs,
        out_specs=ACC_SPEC,
        out_shape=ACC_SHAPE,
        compiler_params=pltpu.CompilerParams(vmem_limit_bytes=limit * 1024 * 1024),
        cost_estimate=cost(0.01),
        name="attend",
    )(*args)


def finish(flags, q, tiles, offset, acc, mixed, out_weight, every):
    specs, args = tile_specs(flags, q, tiles)
    anywhere = pl.BlockSpec(memory_space=pl.ANY)
    arrays, places = [], []
    for k, k_at, v, v_at in every:
        where = []
        for array in (k, v):
            known = [i for i, other in enumerate(arrays) if other is array]
            if not known:
                arrays.append(array)
            where.append(known[0] if known else len(arrays) - 1)
        places.append((where[0], k_at, where[1], v_at))
    specs += [ACC_SPEC, whole(TOKENS, CHANNELS), whole(CHANNELS, CHANNELS)]
    specs += [anywhere] * (1 + len(arrays))
    args += [acc, mixed, out_weight, q] + arrays
    return pl.pallas_call(
        functools.partial(finish_kernel, len(tiles), offset, tuple(places)),
        grid=(PAIRS,),
        in_specs=specs,
        out_specs=whole(TOKENS, CHANNELS),
        out_shape=jax.ShapeDtypeStruct((TOKENS, CHANNELS), BF16),
        scratch_shapes=[
            pltpu.VMEM((1, TOKENS, 256), F32),
            pltpu.VMEM((TOKENS, CHANNELS), BF16),
            pltpu.SMEM((1,), jnp.int32),
            pltpu.VMEM((2, TOKENS, 128), BF16),
            pltpu.VMEM((TOKENS, 128), BF16),
            pltpu.VMEM((TOKENS, 128), BF16),
            pltpu.VMEM((TOKENS, 128), F32),
            pltpu.VMEM((TOKENS, 256), F32),
            pltpu.SemaphoreType.DMA,
        ],
        compiler_params=pltpu.CompilerParams(vmem_limit_bytes=20 * 1024 * 1024),
        cost_estimate=cost(len(tiles)),
        name="finish",
    )(*args)


def body(
    latent,
    stale,
    stale_kv,
    neighbors,
    readers,
    timestep,
    conv_weight,
    time_weight,
    norm_gain,
    qkv_weight,
    out_weight,
):
    tile = stale_kv.reshape(2, TOKENS, CHANNELS)
    weights = conv_weight.reshape(3, 3 * CHANNELS, CHANNELS)
    place = jnp.stack([lax.axis_index("lon"), lax.axis_index("lat")]).astype(jnp.int32)

    left = send(stale[:, -1:], lambda p, band: (p + 1) % N_LON)
    right = send(stale[:, :1], lambda p, band: (p - 1) % N_LON)

    tile, left, right = lax.optimization_barrier((tile, left, right))
    got_r = send(tile, partner)

    masks, wide = prepare(place, neighbors, left, right, stale)

    def choose(moved, base):
        rows = []
        for way in range(2):
            total = moved[0][way].astype(F32) * masks[base + way]
            for step in range(1, len(moved)):
                total += moved[step][way].astype(F32) * masks[base + 2 * step + way]
            rows.append(total.astype(BF16))
        return jnp.stack(rows, 0)

    def shifted(rows):
        x = jnp.concatenate([rows[:, d : d + LON_CELLS] for d in range(3)], -1)
        return x.reshape(-1, 3 * CHANNELS)

    wide = choose([wide] + [send(wide, ring_x(s)) for s in (1, 2, 3)], X_MASKS)
    wide = choose([wide] + [send(wide, ring_z(s)) for s in (1, 2, 3)], Z_MASKS)
    tile, wide, latent, readers, timestep, norm_gain = lax.optimization_barrier(
        (tile, wide, latent, readers, timestep, norm_gain)
    )
    got_f = send(tile, ahead)
    got_b = send(tile, behind)
    acc = conv(left, right, latent, weights)
    lift = jnp.concatenate([time_vector(timestep, time_weight), norm_gain[None, :]], 0)
    flags = flags_of(place, readers)

    wide, acc, got_r, lift, flags = lax.optimization_barrier((wide, acc, got_r, lift, flags))
    both = lambda base: (wide[0].astype(F32) * masks[base] + wide[1].astype(F32) * masks[base + 1]).astype(BF16)
    near = send_band(both(NEAR), ((0, 1), (1, 0), (2, 3), (3, 2)))
    far = send_band(both(FAR), ((1, 2), (2, 1), (0, 0), (3, 3)))
    near, far = near.astype(F32), far.astype(F32)
    wide = jnp.stack(
        [(near * masks[NEAR + 2 + i] + far * masks[FAR + 2 + i]).astype(BF16) for i in range(2)], 0
    )
    swapped = send(wide, partner)
    wide = choose([wide, swapped], Y_MASKS)

    rims = shifted(
        jnp.concatenate(
            [wide[:, LON_CELLS : LON_CELLS + 1], wide[:, :LON_CELLS], wide[:, LON_CELLS + 1 :]], 1
        )
    )
    got_t = send(got_r, ahead, POLAR)
    got_u = send(got_r, behind, POLAR)
    mixed, q, fresh = dense(
        rims,
        weights,
        acc,
        lift,
        latent.reshape(TOKENS, CHANNELS),
        qkv_weight,
    )

    got_b, got_f, q = lax.optimization_barrier((got_b, got_f, q))
    got_s = send(got_b, lambda p, band: aside(p) if band in POLAR else partner(p))
    sums = attend(flags, q, [one(fresh), one(got_r)], 0)
    sums = attend(flags, q, [one(got_f), one(got_b)], 2, sums)
    sums = attend(flags, q, [one(got_t), one(got_u)], 4, sums)
    every = [one(tile) for tile in (fresh, got_r, got_f, got_b, got_t, got_u, got_s)]
    out = finish(flags, q, [one(got_s)], 6, sums, mixed, out_weight, every)
    return (
        out.reshape(LAT_CELLS, LON_CELLS, CHANNELS),
        fresh.reshape(2, LAT_CELLS, LON_CELLS, CHANNELS),
    )


def solution(mesh):
    in_specs = (
        P("lat", "lon", None),
        P("lat", "lon", None),
        P(None, "lat", "lon", None),
        P(),
        P(),
        P(),
        P(),
        P(),
        P(),
        P(),
        P(),
    )
    out_specs = (P("lat", "lon", None), P(None, "lat", "lon", None))
    return jax.shard_map(body, mesh=mesh, in_specs=in_specs, out_specs=out_specs, check_vma=False)
```
